32 devices in a mesh: leaf: 2 (over y), tok: 16 (over z, x, core).
Axes of the slice: x: 2, y: 2, z: 4, core: 2. Of those that a mesh axis runs over, the one named last changes fastest.
Arguments:
- hidden_in: bfloat16 [4, 2048, 1024], P('leaf', 'tok'), may hold values from -7 to 7
- output_cotangent: bfloat16 [4, 2048, 1024], P('leaf', 'tok'), may hold values from -6 to 6
- unit_place: int32 [4, 16], P('leaf'), may hold values from 0 to 15, as said below
- ln1_gain: bfloat16 [1024], P(('leaf', 'tok')), may hold values from 0.25 to 1.75
- ln1_bias: bfloat16 [1024], P(('leaf', 'tok')), may hold values from -1.5 to 1.5
- qkv_weight: bfloat16 [1024, 3072], P(('leaf', 'tok')), may hold values from -0.12617187 to 0.12617187
- qv_bias: bfloat16 [2048], P(('leaf', 'tok')), may hold values from -1.5 to 1.5
- out_weight: bfloat16 [1024, 1024], P(('leaf', 'tok')), may hold values from -0.5 to 0.5
- out_bias: bfloat16 [1024], P(('leaf', 'tok')), may hold values from -1.5 to 1.5
- ln2_gain: bfloat16 [1024], P(('leaf', 'tok')), may hold values from 0.25 to 1.75
- ln2_bias: bfloat16 [1024], P(('leaf', 'tok')), may hold values from -1.5 to 1.5
- fc1_weight: bfloat16 [1024, 4096], P(('leaf', 'tok')), may hold values from -0.1875 to 0.1875
- fc1_bias: bfloat16 [4096], P(('leaf', 'tok')), may hold values from -1.5 to 1.5
- fc2_weight: bfloat16 [4096, 1024], P(('leaf', 'tok')), may hold values from -0.09375 to 0.09375
- fc2_bias: bfloat16 [1024], P(('leaf', 'tok')), may hold values from -1.5 to 1.5
Outputs:
- layer_out: bfloat16 [4, 2048, 1024], P('leaf', 'tok')
- input_grad: bfloat16 [4, 2048, 1024], P('leaf', 'tok')
- ln1_gain_grad: float32 [1024], P(('leaf', 'tok'))
- ln1_bias_grad: float32 [1024], P(('leaf', 'tok'))
- qkv_weight_grad: float32 [1024, 3072], P(('leaf', 'tok'))
- qv_bias_grad: float32 [2048], P(('leaf', 'tok'))
- out_weight_grad: float32 [1024, 1024], P(('leaf', 'tok'))
- out_bias_grad: float32 [1024], P(('leaf', 'tok'))
- ln2_gain_grad: float32 [1024], P(('leaf', 'tok'))
- ln2_bias_grad: float32 [1024], P(('leaf', 'tok'))
- fc1_weight_grad: float32 [1024, 4096], P(('leaf', 'tok'))
- fc1_bias_grad: float32 [4096], P(('leaf', 'tok'))
- fc2_weight_grad: float32 [4096, 1024], P(('leaf', 'tok'))
- fc2_bias_grad: float32 [1024], P(('leaf', 'tok'))
The draws below stay inside these ranges and needn't reach their ends.
Inputs may be any that keep to these rules, and one draw needn't show every extreme that they name: `unit_place`: each row is a permutation of 0 to 15. Units 0 to 3 are the trunk's quarters in order, 4 to 7 the branches, 8 to 15 the leaves; leaf 8 + k hangs from branch 4 + k // 2.
All inputs are finite; a program needn't handle non-finite values.
Results may differ from the reference program's by a relative error of at most 0.0085.
Values may be sent and summed in bfloat16 or wider, within the bound.
No kernel may reach another device: no remote copies, remote signals or barrier semaphores. Data moves between devices by JAX's collectives and lax.ppermute only.
A program may use at most 192 MiB of HBM per device.

```python
import jax
import jax.numpy as jnp
from jax import lax

D = 1024
HEADS = 16
HEAD_DIM = 64
FF = 4096
UNITS = 16
TREE = 2048
TREES = 4


def tree_orders(key):
    order_key = jax.random.fold_in(key, 101)
    tree_keys = jax.random.split(order_key, TREES)
    return jax.vmap(lambda one_key: jax.random.permutation(one_key, UNITS))(tree_keys).astype(jnp.int32)


def shared_signs(key):
    sign_key = jax.random.fold_in(key, 202)
    return jax.random.rademacher(sign_key, (3, D), dtype=jnp.float32)


def draw_unit_place(key, part):
    return tree_orders(key)


def draw_hidden_in(key, part):
    placement = tree_orders(key)
    signs = shared_signs(key)
    key = jax.random.fold_in(key, 3)
    noise = jnp.clip(jax.random.normal(key, (TREES, TREE, D), jnp.float32), -4.0, 4.0)
    unit_len = TREE // UNITS
    slot_index = jnp.arange(TREE, dtype=jnp.int32) // unit_len
    unit_here = placement[:, slot_index]
    root_rows = (unit_here == 0).astype(jnp.float32)
    common = signs[0][None, None, :]
    rooted = 2.0 * root_rows[:, :, None] * signs[1][None, None, :]
    return (noise + common + rooted).astype(jnp.bfloat16)


def draw_qkv_weight(key, part):
    signs = shared_signs(key)
    key = jax.random.fold_in(key, 5)
    base = jnp.clip(jax.random.normal(key, (D, 3 * D), jnp.float32), -4.0, 4.0) * D ** (-0.5)
    head_signs = signs[2]
    query_extra = 1.0 / D * signs[0][:, None] * head_signs[None, :]
    key_extra = 1.2 / D * signs[1][:, None] * head_signs[None, :]
    extra = jnp.concatenate([query_extra, key_extra, jnp.zeros((D, D), jnp.float32)], axis=1)
    return (base + extra).astype(jnp.bfloat16)


def shard_levels(own_key, extent, pieces, smallest, top_value):
    level = 1.0
    for dim, shards_of in pieces:
        steps = jax.random.uniform(jax.random.fold_in(jax.random.fold_in(own_key, 6), dim), (shards_of,), jnp.float32, smallest / len(pieces), top_value / len(pieces))
        level = level * jnp.repeat(jnp.exp(steps), extent[dim] // shards_of).reshape((-1,) + (1,) * (len(extent) - 1 - dim))
    return level


def gaussian(stream_key, dims, scale, limit, cuts=(), kind=jnp.bfloat16):
    values = scale * jax.random.normal(stream_key, dims, jnp.float32)
    if cuts:
        values = values * shard_levels(stream_key, dims, cuts, -0.22, 0.18)
    return jnp.clip(values, -limit, limit).astype(kind)


def setup_inputs(seed: int = 0) -> dict:
    streams_of = jax.random.split(jax.random.key(seed), 16)
    hidden_in = draw_hidden_in(jax.random.fold_in(streams_of[15], 71), 0)
    output_cotangent = gaussian(streams_of[1], (TREES, TREE, D), 1.0, 6.0, ((0, 2), (1, 16)))
    unit_place = draw_unit_place(jax.random.fold_in(streams_of[15], 71), 0)
    ln1_gain = jnp.clip(1.0 + 0.15 * jax.random.normal(streams_of[3], (D,), jnp.float32), 0.25, 1.75).astype(jnp.bfloat16)
    ln1_bias = gaussian(streams_of[4], (D,), 0.3, 1.5, ((0, 32),))
    qkv_weight = draw_qkv_weight(jax.random.fold_in(streams_of[15], 71), 0)
    qv_bias = gaussian(streams_of[6], (2 * D,), 0.3, 1.5, ((0, 32),))
    out_weight = gaussian(streams_of[7], (D, D), (D // 8) ** -0.5, 0.5, ((0, 32),))
    out_bias = gaussian(streams_of[8], (D,), 0.3, 1.5, ((0, 32),))
    ln2_gain = jnp.clip(1.0 + 0.15 * jax.random.normal(streams_of[9], (D,), jnp.float32), 0.25, 1.75).astype(jnp.bfloat16)
    ln2_bias = gaussian(streams_of[10], (D,), 0.3, 1.5, ((0, 32),))
    fc1_weight = gaussian(streams_of[11], (D, FF), D ** -0.5, 0.1875, ((0, 32),))
    fc1_bias = gaussian(streams_of[12], (FF,), 0.3, 1.5, ((0, 32),))
    fc2_weight = gaussian(streams_of[13], (FF, D), FF ** -0.5, 0.09375, ((0, 32),))
    fc2_bias = gaussian(streams_of[14], (D,), 0.3, 1.5, ((0, 32),))
    return dict(hidden_in=hidden_in, output_cotangent=output_cotangent, unit_place=unit_place, ln1_gain=ln1_gain, ln1_bias=ln1_bias, qkv_weight=qkv_weight, qv_bias=qv_bias, out_weight=out_weight, out_bias=out_bias, ln2_gain=ln2_gain, ln2_bias=ln2_bias, fc1_weight=fc1_weight, fc1_bias=fc1_bias, fc2_weight=fc2_weight, fc2_bias=fc2_bias)


@jax.custom_vjp
def low(v):
    return lax.optimization_barrier(v.astype(jnp.bfloat16)).astype(jnp.float32)

@jax.custom_vjp
def low_back(v):
    return v

def low_keep(v):
    return (low(v), None)

def low_pass(kept, grad):
    return (grad,)

def back_keep(v):
    return (v, None)

def back_low(kept, grad):
    return (low(grad),)
low.defvjp(low_keep, low_pass)
low_back.defvjp(back_keep, back_low)
layer_eps = 1e-05
masked_score = -1e+30

def layer_norm(values, gain_vec, shift_vec):
    row_mean = lax.optimization_barrier(jnp.mean(values, axis=-1, keepdims=True))
    centered = values - row_mean
    spread = lax.optimization_barrier(jnp.mean(centered * centered, axis=-1, keepdims=True))
    return centered * lax.rsqrt(spread + layer_eps) * gain_vec + shift_vec

def matmul_high(left, right):
    return jnp.dot(left, right, precision=lax.Precision.HIGHEST)

def tree_layout(placement):
    unit_len = TREE // UNITS
    position = jnp.arange(TREE, dtype=jnp.int32)
    slot_index = position // unit_len
    within = position - slot_index * unit_len
    picked = slot_index[:, None] == jnp.arange(UNITS, dtype=jnp.int32)[None, :]
    chosen = lax.optimization_barrier(jnp.sum(jnp.where(picked, placement[None, :], 0), axis=1)).astype(jnp.int32)
    offset = jnp.where(chosen < 4, chosen * unit_len, jnp.where(chosen < 8, 4 * unit_len, 5 * unit_len))
    branches = jnp.where(chosen < 4, -1, jnp.where(chosen < 8, chosen - 4, (chosen - 8) // 2))
    leaves = jnp.where(chosen < 8, -1, chosen - 8)
    return ((offset + within).astype(jnp.int32), branches.astype(jnp.int32), leaves.astype(jnp.int32))

def attend(query_heads, key_heads, value_heads, depths, branches, leaves):
    block_size = min(512, TREE)
    head_slopes = jnp.power(2.0, -8.0 * (jnp.arange(HEADS, dtype=jnp.float32) + 1.0) / HEADS)
    score_scale = HEAD_DIM ** (-0.5)

    def one_block(block_index):
        first_row = block_index * block_size
        query_rows = lax.dynamic_slice_in_dim(query_heads, first_row, block_size, 0)
        query_depth = lax.dynamic_slice_in_dim(depths, first_row, block_size, 0)
        query_branch = lax.dynamic_slice_in_dim(branches, first_row, block_size, 0)
        query_leaf = lax.dynamic_slice_in_dim(leaves, first_row, block_size, 0)
        raw_scores = low_back(jnp.einsum('qhe,khe->hqk', query_rows, key_heads, precision=lax.Precision.HIGHEST) * score_scale)
        same_branch = (branches[None, :] < 0) | (branches[None, :] == query_branch[:, None])
        same_leaf = (leaves[None, :] < 0) | (leaves[None, :] == query_leaf[:, None])
        allowed = same_branch & same_leaf & (depths[None, :] <= query_depth[:, None])
        distance = (query_depth[:, None] - depths[None, :]).astype(jnp.float32)
        scores = raw_scores - head_slopes[:, None, None] * distance[None, :, :]
        scores = jnp.where(allowed[None, :, :], scores, masked_score)
        log_total = jax.nn.logsumexp(scores, axis=-1, keepdims=True)
        probs = low(jnp.exp(scores - log_total))
        return jnp.einsum('hqk,khe->qhe', probs, value_heads, precision=lax.Precision.HIGHEST)
    block_outs = lax.map(jax.checkpoint(one_block), jnp.arange(TREE // block_size, dtype=jnp.int32))
    return block_outs.reshape(TREE, HEADS * HEAD_DIM)

def tree_forward(weights, hidden, placement):
    gain_one, shift_one, w_mixed, bias_mixed, w_output, bias_output, gain_two, shift_two, up_weight, bias_expand, down_weight, bias_reduce = weights
    depths, branches, leaves = tree_layout(placement)
    normed_one = low(layer_norm(hidden, gain_one, shift_one))
    projected = matmul_high(normed_one, w_mixed)
    queries = low_back(low(projected[:, :D] + bias_mixed[:D]))
    key_rows = low_back(low(projected[:, D:2 * D]))
    values = low_back(low(projected[:, 2 * D:] + bias_mixed[D:]))
    context = attend(queries.reshape(TREE, HEADS, HEAD_DIM), key_rows.reshape(TREE, HEADS, HEAD_DIM), values.reshape(TREE, HEADS, HEAD_DIM), depths, branches, leaves)
    context = low_back(low(context))
    branch_out = low_back(matmul_high(context, w_output) + bias_output)
    middle = hidden + branch_out
    second_normalized = low(layer_norm(middle, gain_two, shift_two))
    expand = low_back(matmul_high(second_normalized, up_weight) + bias_expand)
    activated_hidden = low(jax.nn.gelu(expand, approximate=True))
    reduced = low_back(matmul_high(activated_hidden, down_weight) + bias_reduce)
    return middle + reduced

def reference(hidden_in, output_cotangent, unit_place, ln1_gain, ln1_bias, qkv_weight, qv_bias, out_weight, out_bias, ln2_gain, ln2_bias, fc1_weight, fc1_bias, fc2_weight, fc2_bias):
    weights = tuple((item.astype(jnp.float32) for item in (ln1_gain, ln1_bias, qkv_weight, qv_bias, out_weight, out_bias, ln2_gain, ln2_bias, fc1_weight, fc1_bias, fc2_weight, fc2_bias)))
    hidden = hidden_in.astype(jnp.float32)
    cotangent = output_cotangent.astype(jnp.float32)
    checked = jax.checkpoint(tree_forward)

    def forward(weight_set, inputs):

        def step_tree(carry, entries):
            tree_in, placement = entries
            return (carry, checked(weight_set, tree_in, placement))
        unused, outputs = lax.scan(step_tree, jnp.zeros((), jnp.float32), (inputs, unit_place))
        return outputs
    result, pullback = jax.vjp(forward, weights, hidden)
    weight_grads, input_grad = pullback(cotangent)
    g_gain_one, g_shift_one, g_w_mixed, g_b_mixed, g_w_output, g_b_output, g_gain_two, g_shift_two, g_w_expand, g_b_expand, down_weight_gradient, g_b_reduce = weight_grads
    return (result.astype(jnp.bfloat16), input_grad.astype(jnp.bfloat16), g_gain_one, g_shift_one, g_w_mixed, g_b_mixed, g_w_output, g_b_output, g_gain_two, g_shift_two, g_w_expand, g_b_expand, down_weight_gradient, g_b_reduce)
```

```python
import jax
import jax.numpy as jnp
from jax import lax
from jax.experimental import pallas as pl
from jax.experimental.pallas import tpu as pltpu
from jax.sharding import PartitionSpec as P

HEADS = 16
UNITS = 16
LOG2E = 1.4426950408889634

layer_eps = 1e-05
masked_score = -1e30
f32 = jnp.float32
bf16 = jnp.bfloat16


def normalize(values):
    row_mean = jnp.mean(values, axis=-1, keepdims=True)
    centered = values - row_mean
    spread = jnp.mean(centered * centered, axis=-1, keepdims=True)
    inverse = lax.rsqrt(spread + layer_eps)
    return centered * inverse, inverse


def norm_back(hat, inverse, gain, grad):
    scaled = grad * gain
    first = jnp.mean(scaled, axis=-1, keepdims=True)
    second = jnp.mean(scaled * hat, axis=-1, keepdims=True)
    return (scaled - first - hat * second) * inverse


def unit_pieces(unit_kind, unit_len):
    if unit_kind < 4:
        return unit_kind
    return 4


def fill_units(pos_ref, qkv_ref, scratches, width):
    blocks, rows, _ = qkv_ref.shape
    for i in range(blocks):
        dst = pl.ds(pl.multiple_of(pos_ref[i], rows), rows)
        for n, scratch in enumerate(scratches):
            scratch[dst, :] = qkv_ref[i, :, n * width : (n + 1) * width]


def fill_transposed(src, dst, unit_len):
    for u in range(UNITS):
        dst[:, u * unit_len : (u + 1) * unit_len] = (
            src[u * unit_len : (u + 1) * unit_len, :].astype(f32).T.astype(bf16)
        )


def head_stack(block, heads, head_size):
    if heads == 1:
        return block
    lane = lax.broadcasted_iota(jnp.int32, block.shape, 1) // head_size
    return jnp.concatenate(
        [jnp.where(lane == h, block, jnp.zeros_like(block)) for h in range(heads)], axis=0
    )


def fill_bias(slope_ref, bias_ref, heads, unit_len):
    depth = lax.broadcasted_iota(jnp.int32, (bias_ref.shape[0], unit_len), 0).astype(f32)
    for h in range(heads):
        bias_ref[:, h * unit_len : (h + 1) * unit_len] = depth * slope_ref[h]


def nt_dot(left, right):
    return lax.dot_general(left, right, (((1,), (1,)), ((), ())), preferred_element_type=f32)


def nn_dot(left, right):
    return lax.dot_general(left, right, (((1,), (0,)), ((), ())), preferred_element_type=f32)


def diag_of(wide, heads, head_size, unit_len):
    return jnp.concatenate(
        [
            wide[h * head_size : (h + 1) * head_size, h * unit_len : (h + 1) * unit_len]
            for h in range(heads)
        ],
        axis=0,
    )


def over_units(unit_len, one_unit):
    for u in range(4):
        pieces = [(u * unit_len, unit_len, u * unit_len, True)]
        if u:
            pieces = [(0, u * unit_len, 0, False)] + pieces
        one_unit(u * unit_len, pieces)

    def branch(b, carry):
        start = pl.multiple_of((4 + b) * unit_len, unit_len)
        one_unit(
            start, [(0, 4 * unit_len, 0, False), (start, unit_len, 4 * unit_len, True)]
        )
        return carry

    lax.fori_loop(0, 4, branch, 0)

    def leaf(k, carry):
        start = pl.multiple_of((8 + k) * unit_len, unit_len)
        parent = pl.multiple_of((4 + k // 2) * unit_len, unit_len)
        one_unit(
            start,
            [
                (0, 4 * unit_len, 0, False),
                (parent, unit_len, 4 * unit_len, False),
                (start, unit_len, 5 * unit_len, True),
            ],
        )
        return carry

    lax.fori_loop(0, 8, leaf, 0)


def forward_kernel(
    pos_ref, out_pos_ref, slope_ref, qkv_ref, ctx_ref, log_ref, q_s, k_s, v_s, vt_s, bias_s, c_s,
    *, heads, head_size
):
    width = heads * head_size
    unit_len = q_s.shape[0] // UNITS
    blocks, rows, _ = qkv_ref.shape
    fill_units(pos_ref, qkv_ref, (q_s, k_s, v_s), width)
    fill_transposed(v_s, vt_s, unit_len)
    fill_bias(slope_ref, bias_s, heads, unit_len)
    scale = head_size ** (-0.5) * LOG2E
    columns = heads * unit_len
    key_row = lax.broadcasted_iota(jnp.int32, (unit_len, columns), 0)
    query_col = lax.broadcasted_iota(jnp.int32, (unit_len, columns), 1) % unit_len
    causal = key_row <= query_col

    def one_unit(start, pieces):
        stacked = head_stack(q_s[pl.ds(start, unit_len), :], heads, head_size)
        scores = []
        top = None
        for key_start, size, depth, diagonal in pieces:
            s = nt_dot(k_s[pl.ds(key_start, size), :], stacked) * scale
            s = s + bias_s[depth : depth + size, :]
            if diagonal:
                s = jnp.where(causal, s, masked_score)
            scores.append(s)
            m = jnp.max(s, axis=0, keepdims=True)
            top = m if top is None else jnp.maximum(top, m)
        total = None
        wide = None
        for (key_start, size, depth, diagonal), s in zip(pieces, scores):
            p = jnp.exp2(s - top)
            part = jnp.sum(p, axis=0, keepdims=True)
            total = part if total is None else total + part
            o = nn_dot(vt_s[:, pl.ds(key_start, size)], p.astype(bf16))
            wide = o if wide is None else wide + o
        wide = wide * (1.0 / total)
        log_ref[pl.ds(start // unit_len, 1), :] = top + jnp.log2(total)
        c_s[pl.ds(start, unit_len), :] = diag_of(wide, heads, head_size, unit_len).T.astype(bf16)

    over_units(unit_len, one_unit)
    for i in range(blocks):
        src = pl.ds(pl.multiple_of(pos_ref[i], rows), rows)
        ctx_ref[out_pos_ref[i], :, :] = c_s[src, :]


def backward_kernel(
    pos_ref, out_pos_ref, slope_ref, qkv_ref, log_ref, gctx_ref, out_ref,
    q_s, k_s, v_s, kt_s, g_s, bias_s, dq_s, dk_s, dv_s, *, heads, head_size
):
    width = heads * head_size
    unit_len = q_s.shape[0] // UNITS
    blocks, rows, _ = qkv_ref.shape
    fill_units(pos_ref, qkv_ref, (q_s, k_s, v_s), width)
    for i in range(blocks):
        dst = pl.ds(pl.multiple_of(pos_ref[i], rows), rows)
        g_s[dst, :] = gctx_ref[out_pos_ref[i], :, :]
    fill_transposed(k_s, kt_s, unit_len)
    fill_bias(slope_ref, bias_s, heads, unit_len)
    dk_s[...] = jnp.zeros_like(dk_s)
    dv_s[...] = jnp.zeros_like(dv_s)
    size_scale = head_size ** (-0.5)
    scale = size_scale * LOG2E
    columns = heads * unit_len
    key_row = lax.broadcasted_iota(jnp.int32, (unit_len, columns), 0)
    query_col = lax.broadcasted_iota(jnp.int32, (unit_len, columns), 1) % unit_len
    causal = key_row <= query_col

    def one_unit(start, pieces):
        stacked = head_stack(q_s[pl.ds(start, unit_len), :], heads, head_size)
        grads = head_stack(g_s[pl.ds(start, unit_len), :], heads, head_size)
        log_total = log_ref[pl.ds(start // unit_len, 1), :]
        kept = []
        delta = None
        for key_start, size, depth, diagonal in pieces:
            s = nt_dot(k_s[pl.ds(key_start, size), :], stacked) * scale
            s = s + bias_s[depth : depth + size, :]
            if diagonal:
                s = jnp.where(causal, s, masked_score)
            p = jnp.exp2(s - log_total)
            gp = nt_dot(v_s[pl.ds(key_start, size), :], grads)
            kept.append((p, gp))
            part = jnp.sum(p * gp, axis=0, keepdims=True)
            delta = part if delta is None else delta + part
        wide = None
        for (key_start, size, depth, diagonal), (p, gp) in zip(pieces, kept):
            ds = (p * (gp - delta)).astype(bf16)
            keys = pl.ds(key_start, size)
            dv_s[keys, :] += nn_dot(p.astype(bf16), grads)
            dk_s[keys, :] += nn_dot(ds, stacked)
            o = nn_dot(kt_s[:, keys], ds)
            wide = o if wide is None else wide + o
        dq = diag_of(wide, heads, head_size, unit_len).T * size_scale
        dq_s[pl.ds(start, unit_len), :] = dq.astype(bf16)

    over_units(unit_len, one_unit)
    for i in range(blocks):
        src = pl.ds(pl.multiple_of(pos_ref[i], rows), rows)
        out_ref[i, :, :width] = dq_s[src, :]
        out_ref[i, :, width : 2 * width] = (dk_s[src, :] * size_scale).astype(bf16)
        out_ref[i, :, 2 * width :] = dv_s[src, :].astype(bf16)


def attention_forward(pos, out_pos, slopes, qkv, heads, head_size):
    blocks, rows, _ = qkv.shape
    tokens, width = blocks * rows, heads * head_size
    unit_len = tokens // UNITS
    smem = pl.BlockSpec(memory_space=pltpu.SMEM)
    vmem = pl.BlockSpec(memory_space=pltpu.VMEM)
    seq = lambda: pltpu.VMEM((tokens, width), bf16)
    return pl.pallas_call(
        lambda *refs: forward_kernel(*refs, heads=heads, head_size=head_size),
        out_shape=(
            jax.ShapeDtypeStruct((blocks, rows, width), bf16),
            jax.ShapeDtypeStruct((UNITS, heads * unit_len), f32),
        ),
        in_specs=[smem, smem, smem, vmem],
        out_specs=(vmem, vmem),
        scratch_shapes=[
            seq(), seq(), seq(), pltpu.VMEM((width, tokens), bf16),
            pltpu.VMEM((6 * unit_len, heads * unit_len), f32), seq(),
        ],
        compiler_params=pltpu.CompilerParams(vmem_limit_bytes=24 * 2**20),
        cost_estimate=pl.CostEstimate(
            flops=tokens * tokens * width * 2, bytes_accessed=tokens * width * 16,
            transcendentals=tokens * tokens * heads // 3,
        ),
    )(pos, out_pos, slopes, qkv)


def attention_backward(pos, out_pos, slopes, qkv, log_total, gctx, heads, head_size):
    blocks, rows, _ = qkv.shape
    tokens, width = blocks * rows, heads * head_size
    unit_len = tokens // UNITS
    smem = pl.BlockSpec(memory_space=pltpu.SMEM)
    vmem = pl.BlockSpec(memory_space=pltpu.VMEM)
    seq = lambda: pltpu.VMEM((tokens, width), bf16)
    acc = lambda: pltpu.VMEM((tokens, width), f32)
    return pl.pallas_call(
        lambda *refs: backward_kernel(*refs, heads=heads, head_size=head_size),
        out_shape=jax.ShapeDtypeStruct((blocks, rows, 3 * width), bf16),
        in_specs=[smem, smem, smem, vmem, vmem, vmem],
        out_specs=vmem,
        scratch_shapes=[
            seq(), seq(), seq(), pltpu.VMEM((width, tokens), bf16), seq(),
            pltpu.VMEM((6 * unit_len, heads * unit_len), f32), seq(), acc(), acc(),
        ],
        compiler_params=pltpu.CompilerParams(vmem_limit_bytes=32 * 2**20),
        cost_estimate=pl.CostEstimate(
            flops=tokens * tokens * width * 5, bytes_accessed=tokens * width * 30,
            transcendentals=tokens * tokens * heads // 3,
        ),
    )(pos, out_pos, slopes, qkv, log_total, gctx)


def swap(values, axis, mask):
    size = lax.axis_size(axis)
    return lax.ppermute(values, axis, [(i, i ^ mask) for i in range(size)])


def masks_of(size):
    found, mask = [], 1
    while mask < size:
        found.append(mask)
        mask *= 2
    return found


def grow(values, axis, masks):
    index = lax.axis_index(axis)
    for mask in masks:
        other = swap(values, axis, mask)
        high = (index & mask) != 0
        values = jnp.concatenate(
            [jnp.where(high, other, values), jnp.where(high, values, other)], axis=0
        )
    return values


def shrink(values, axis, masks):
    index = lax.axis_index(axis)
    for mask in reversed(masks):
        half = values.shape[0] // 2
        low, high = values[:half], values[half:]
        upper = (index & mask) != 0
        other = swap(jnp.where(upper, low, high), axis, mask)
        values = (
            jnp.where(upper, high, low).astype(f32) + other.astype(f32)
        ).astype(values.dtype)
    return values


def block_order(ranks):
    far = [m for m in masks_of(ranks) if m > 1]
    order = []
    for half, masks in ((0, far), (1, far[::-1])):
        seen = [0]
        for m in masks:
            seen = seen + [j ^ m for j in seen]
        order += [(j, half) for j in seen]
    return order + [(j ^ 1, half) for j, half in order]


def gather_blocks(pair, ranks):
    far = [m for m in masks_of(ranks) if m > 1]
    halves = []
    for half, masks in ((0, far), (1, far[::-1])):
        held = pair[half : half + 1]
        for m in masks:
            held = jnp.concatenate([held, swap(held, "tok", m)], axis=0)
        halves.append(held)
    held = jnp.concatenate(halves, axis=0)
    return jnp.concatenate([held, swap(held, "tok", 1)], axis=0)


def scatter_blocks(partial, ranks):
    far = [m for m in masks_of(ranks) if m > 1]
    n = partial.shape[0] // 2
    other = swap(partial[n:].astype(bf16), "tok", 1)
    held = partial[:n].astype(f32) + other.astype(f32)
    done = []
    for half, masks in ((0, far), (1, far[::-1])):
        part = held[half * (n // 2) : (half + 1) * (n // 2)]
        for m in masks[::-1]:
            k = part.shape[0] // 2
            part = part[:k] + swap(part[k:].astype(bf16), "tok", m).astype(f32)
        done.append(part)
    return jnp.concatenate(done, axis=0)


def on_device(
    hidden_in, output_cotangent, unit_place, ln1_gain, ln1_bias, qkv_weight, qv_bias, out_weight,
    out_bias, ln2_gain, ln2_bias, fc1_weight, fc1_bias, fc2_weight, fc2_bias,
):
    trees, rows, width = hidden_in.shape
    tok_size, leaf_size = lax.axis_size("tok"), lax.axis_size("leaf")
    ranks = tok_size // trees
    head_size = width // HEADS
    heads = HEADS // ranks
    lanes = heads * head_size
    hidden_units = fc1_weight.shape[1]
    own_units = fc1_bias.shape[0]
    weight_rows = qkv_weight.shape[0]
    groups = leaf_size * trees
    tokens = rows * tok_size
    unit_len = tokens // UNITS
    leaf_masks, tree_masks = masks_of(leaf_size), [m * ranks for m in masks_of(trees)]
    index = lax.axis_index("tok")
    tree, rank = index // ranks, index % ranks
    rank_groups = [[g * ranks + i for i in range(ranks)] for g in range(trees)]

    def exchange(values):
        mine = jnp.where(tree == 0, values[0], values[1])
        other = swap(jnp.where(tree == 0, values[1], values[0]), "tok", ranks)
        return jnp.stack([jnp.where(tree == 0, mine, other), jnp.where(tree == 0, other, mine)])

    def to_ranks(values):
        return lax.all_to_all(
            values, "tok", 0, 0, tiled=True, axis_index_groups=rank_groups
        )

    def spread(values):
        return grow(grow(values[None], "tok", tree_masks), "leaf", leaf_masks)

    def collect(values):
        return shrink(shrink(values, "leaf", leaf_masks), "tok", tree_masks)[0]

    order = block_order(ranks)
    dist = jnp.array([j for j, _ in order], jnp.int32)
    half = jnp.array([h for _, h in order], jnp.int32)
    peer = rank ^ dist
    position = (half * ranks + peer) * rows
    place = jnp.where(tree == 0, unit_place[0], unit_place[1])
    slot = position // unit_len
    unit_at = jnp.sum(
        jnp.where(slot[:, None] == jnp.arange(UNITS, dtype=jnp.int32)[None, :], place[None, :], 0),
        axis=1,
    )
    pos = unit_at * unit_len + position % unit_len
    out_pos = peer * 2 + half
    head_index = (rank * heads + jnp.arange(heads, dtype=jnp.int32)).astype(f32)
    slopes = jnp.exp2(-8.0 * (head_index + 1.0) / HEADS) * LOG2E

    hidden = exchange(hidden_in)
    hidden_all = gather_blocks(hidden, ranks)

    small = jnp.concatenate(
        [ln1_gain, ln1_bias, qv_bias, out_bias, ln2_gain, ln2_bias, fc1_bias, fc2_bias]
    )
    mixed_cols = 3 * lanes
    small_rows = -(-small.shape[0] // mixed_cols)
    small_block = jnp.pad(small, (0, small_rows * mixed_cols - small.shape[0]))
    small_block = jnp.broadcast_to(
        small_block.reshape(1, small_rows, mixed_cols), (ranks, small_rows, mixed_cols)
    )
    mixed_parts = (
        qkv_weight.reshape(weight_rows, 3, ranks, lanes)
        .transpose(2, 0, 1, 3)
        .reshape(ranks, weight_rows, mixed_cols)
    )
    up_cols = groups * own_units
    up_parts = (
        fc1_weight.reshape(weight_rows, groups, ranks, own_units)
        .transpose(2, 0, 1, 3)
        .reshape(ranks, weight_rows, up_cols)
    )
    mixed_sent = to_ranks(jnp.concatenate([mixed_parts, small_block], axis=1))
    up_sent = to_ranks(up_parts)
    mixed_all = spread(mixed_sent)
    w_mixed = mixed_all[:, :, :weight_rows].reshape(width, mixed_cols)
    smalls = mixed_all[:, :, weight_rows:].reshape(groups * ranks, small_rows * mixed_cols)
    up_weight = spread(up_sent).reshape(width, up_cols)
    down_weight = spread(fc2_weight).reshape(up_cols, width)
    w_output = lax.all_gather(out_weight, ("leaf", "tok"), axis=0, tiled=True)

    def small_of(start, array):
        n = array.shape[0]
        return smalls[:, start : start + n].reshape(-1).astype(f32), start + n

    gain_one, at = small_of(0, ln1_gain)
    shift_one, at = small_of(at, ln1_bias)
    bias_mixed, at = small_of(at, qv_bias)
    bias_output, at = small_of(at, out_bias)
    gain_two, at = small_of(at, ln2_gain)
    shift_two, at = small_of(at, ln2_bias)
    bias_up, at = small_of(at, fc1_bias)
    bias_down, at = small_of(at, fc2_bias)
    own_bias_up = lax.dynamic_index_in_dim(
        bias_up.reshape(groups, ranks, own_units), rank, 1, keepdims=False
    ).reshape(up_cols)
    query_bias = lax.dynamic_slice_in_dim(bias_mixed, rank * lanes, lanes)
    value_bias = lax.dynamic_slice_in_dim(bias_mixed, width + rank * lanes, lanes)

    cotangent = exchange(output_cotangent)
    cotangent_all = gather_blocks(cotangent, ranks)

    hat_one, inverse_one = normalize(hidden_all.astype(f32))
    normed_one = (hat_one * gain_one + shift_one).astype(bf16)
    projected = jnp.einsum("brd,de->bre", normed_one, w_mixed, preferred_element_type=f32)
    qkv_bias = jnp.concatenate([query_bias, jnp.zeros((lanes,), f32), value_bias])
    qkv = (projected + qkv_bias).astype(bf16)
    ctx_sent, log_total = attention_forward(pos, out_pos, slopes, qkv, heads, head_size)
    ctx_parts = to_ranks(ctx_sent.reshape(ranks, 2 * rows, lanes))
    context = ctx_parts.transpose(1, 0, 2).reshape(2, rows, width)

    branch_out = jnp.einsum("mrd,de->mre", context, w_output, preferred_element_type=f32)
    middle = hidden.astype(f32) + (branch_out + bias_output)
    hat_two, inverse_two = normalize(middle)
    normed_two = (hat_two * gain_two + shift_two).astype(bf16)
    normed_all = gather_blocks(normed_two, ranks)

    expand = jnp.einsum("brd,df->brf", normed_all, up_weight, preferred_element_type=f32)
    expand = expand + own_bias_up
    root = (2.0 / jnp.pi) ** 0.5
    square = expand * expand
    tanh = jnp.tanh(root * (expand + 0.044715 * square * expand))
    active = (0.5 * expand * (1.0 + tanh)).astype(bf16)
    slope = 0.5 * (1.0 + tanh) + 0.5 * expand * (1.0 - tanh * tanh) * root * (
        1.0 + 3 * 0.044715 * square
    )
    grad_active = jnp.einsum("brd,fd->brf", cotangent_all, down_weight, preferred_element_type=f32)
    grad_expand = (grad_active * slope).astype(bf16)
    grad_normed_part = jnp.einsum(
        "brf,df->brd", grad_expand, up_weight, preferred_element_type=f32
    ).astype(bf16)
    grad_normed_two = scatter_blocks(grad_normed_part, ranks)

    reduced_part = jnp.einsum(
        "brf,fd->brd", active, down_weight, preferred_element_type=f32
    ).astype(bf16)
    reduced = scatter_blocks(reduced_part, ranks)
    layer_out = exchange((middle + (reduced + bias_down)).astype(bf16))

    g_down = jnp.einsum("brf,brd->fd", active, cotangent_all, preferred_element_type=f32)
    g_up = jnp.einsum("brd,brf->df", normed_all, grad_expand, preferred_element_type=f32)
    g_bias_up = jnp.sum(grad_expand, axis=(0, 1), dtype=f32)
    g_down_own = collect(g_down.reshape(groups, own_units, width).astype(bf16)).astype(f32)
    g_up_parts = collect(g_up.reshape(groups, ranks, weight_rows, up_cols).astype(bf16))
    g_up_own = (
        to_ranks(g_up_parts)
        .reshape(ranks, weight_rows, groups, own_units)
        .transpose(1, 2, 0, 3)
        .reshape(weight_rows, hidden_units)
        .astype(f32)
    )

    cot = cotangent.astype(f32)
    g_gain_two = jnp.sum(grad_normed_two * hat_two, axis=(0, 1))
    g_shift_two = jnp.sum(grad_normed_two, axis=(0, 1))
    g_bias_down = jnp.sum(cot, axis=(0, 1))
    grad_middle = cot + norm_back(hat_two, inverse_two, gain_two, grad_normed_two)
    grad_branch = grad_middle.astype(bf16)
    g_bias_output = jnp.sum(grad_branch, axis=(0, 1), dtype=f32)
    grad_context = jnp.einsum(
        "mre,de->mrd", grad_branch, w_output, preferred_element_type=f32
    ).astype(bf16)
    gctx_sent = grad_context.reshape(2 * rows, ranks, lanes).transpose(1, 0, 2)
    gctx_parts = to_ranks(gctx_sent).reshape(2 * ranks, rows, lanes)
    g_output = jnp.einsum("mrd,mre->de", context, grad_branch, preferred_element_type=f32)
    g_output_own = lax.psum_scatter(
        g_output.astype(bf16), ("leaf", "tok"), scatter_dimension=0, tiled=True
    ).astype(f32)

    grad_projected = attention_backward(
        pos, out_pos, slopes, qkv, log_total, gctx_parts, heads, head_size
    )
    grad_normed_one = jnp.einsum(
        "bre,de->brd", grad_projected, w_mixed, preferred_element_type=f32
    )
    g_gain_one = jnp.sum(grad_normed_one * hat_one, axis=(0, 1))
    g_shift_one = jnp.sum(grad_normed_one, axis=(0, 1))
    grad_one = scatter_blocks(grad_normed_one.astype(bf16), ranks)
    hat_own, inverse_own = normalize(hidden.astype(f32))
    input_grad = exchange(
        (grad_middle + norm_back(hat_own, inverse_own, gain_one, grad_one)).astype(bf16)
    )

    g_mixed = jnp.einsum("brd,bre->de", normed_one, grad_projected, preferred_element_type=f32)
    g_bias_mixed = jnp.sum(grad_projected, axis=(0, 1), dtype=f32)
    own_lane = jnp.arange(ranks, dtype=jnp.int32)[:, None] == rank
    g_bias_query = jnp.where(own_lane, g_bias_mixed[None, :lanes], 0.0).reshape(-1)
    g_bias_value = jnp.where(own_lane, g_bias_mixed[None, 2 * lanes :], 0.0).reshape(-1)
    g_bias_up_all = jnp.where(
        own_lane[None], g_bias_up.reshape(groups, 1, own_units), 0.0
    ).reshape(-1)
    pieces = [
        g_gain_one, g_shift_one, jnp.concatenate([g_bias_query, g_bias_value]), g_bias_output,
        g_gain_two, g_shift_two, g_bias_up_all, g_bias_down,
    ]
    sizes = [p.shape[0] // (groups * ranks) for p in pieces]
    g_small = jnp.concatenate([p.reshape(groups, ranks, -1) for p in pieces], axis=2)
    g_small = jnp.pad(g_small, ((0, 0), (0, 0), (0, small_rows * mixed_cols - g_small.shape[2])))
    g_sent = jnp.concatenate(
        [
            g_mixed.reshape(groups, ranks, weight_rows, mixed_cols),
            g_small.reshape(groups, ranks, small_rows, mixed_cols),
        ],
        axis=2,
    ).astype(bf16)
    g_back = to_ranks(collect(g_sent))
    g_mixed_own = (
        g_back[:, :weight_rows]
        .reshape(ranks, weight_rows, 3, lanes)
        .transpose(1, 2, 0, 3)
        .reshape(weight_rows, 3 * width)
        .astype(f32)
    )
    small_sum = jnp.sum(g_back[:, weight_rows:].astype(f32), axis=0).reshape(-1)
    found, at = [], 0
    for size in sizes:
        found.append(small_sum[at : at + size])
        at += size
    (
        o_gain_one, o_shift_one, o_bias_mixed, o_bias_output, o_gain_two, o_shift_two, o_bias_up,
        o_bias_down,
    ) = found
    return (
        layer_out, input_grad, o_gain_one, o_shift_one, g_mixed_own, o_bias_mixed, g_output_own,
        o_bias_output, o_gain_two, o_shift_two, g_up_own, o_bias_up, g_down_own, o_bias_down,
    )


def solution(mesh):
    both = ("leaf", "tok")
    tokens, matrix, vector = P("leaf", "tok", None), P(both, None), P(both)
    return jax.shard_map(
        on_device,
        mesh=mesh,
        in_specs=(
            tokens, tokens, P("leaf", None), vector, vector, matrix, vector, matrix, vector, vector,
            vector, matrix, vector, matrix, vector,
        ),
        out_specs=(
            tokens, tokens, vector, vector, matrix, vector, matrix, vector, vector, vector, matrix,
            vector, matrix, vector,
        ),
        check_vma=False,
    )
```

```python
import jax
import jax.numpy as jnp
from jax import lax
from jax.experimental import pallas as pl
from jax.experimental.pallas import tpu as pltpu
from jax.sharding import PartitionSpec as P

HEADS = 16
UNITS = 16
LOG2E = 1.4426950408889634

layer_eps = 1e-05
masked_score = -1e30
f32 = jnp.float32
bf16 = jnp.bfloat16


def normalize(values):
    row_mean = jnp.mean(values, axis=-1, keepdims=True)
    centered = values - row_mean
    spread = jnp.mean(centered * centered, axis=-1, keepdims=True)
    inverse = lax.rsqrt(spread + layer_eps)
    return centered * inverse, inverse


def norm_back(hat, inverse, gain, grad):
    scaled = grad * gain
    first = jnp.mean(scaled, axis=-1, keepdims=True)
    second = jnp.mean(scaled * hat, axis=-1, keepdims=True)
    return (scaled - first - hat * second) * inverse


def fill_transposed(src, dst, unit_len):
    for u in range(UNITS):
        dst[:, u * unit_len : (u + 1) * unit_len] = (
            src[u * unit_len : (u + 1) * unit_len, :].astype(f32).T.astype(bf16)
        )


def head_stack(block, heads, head_size):
    if heads == 1:
        return block
    lane = lax.broadcasted_iota(jnp.int32, block.shape, 1) // head_size
    return jnp.concatenate(
        [jnp.where(lane == h, block, jnp.zeros_like(block)) for h in range(heads)], axis=0
    )


def fill_bias(slope_ref, bias_ref, heads, unit_len):
    depth = lax.broadcasted_iota(jnp.int32, (bias_ref.shape[0], unit_len), 0).astype(f32)
    for h in range(heads):
        bias_ref[:, h * unit_len : (h + 1) * unit_len] = depth * slope_ref[h]


def nt_dot(left, right):
    return lax.dot_general(left, right, (((1,), (1,)), ((), ())), preferred_element_type=f32)


def nn_dot(left, right):
    return lax.dot_general(left, right, (((1,), (0,)), ((), ())), preferred_element_type=f32)


def diag_of(wide, heads, head_size, unit_len):
    return jnp.concatenate(
        [
            wide[h * head_size : (h + 1) * head_size, h * unit_len : (h + 1) * unit_len]
            for h in range(heads)
        ],
        axis=0,
    )


def over_units(unit_len, one_unit):
    for u in range(4):
        pieces = [(u * unit_len, unit_len, u * unit_len, True)]
        if u:
            pieces = [(0, u * unit_len, 0, False)] + pieces
        one_unit(u * unit_len, pieces)

    def branch(b, carry):
        start = pl.multiple_of((4 + b) * unit_len, unit_len)
        one_unit(
            start, [(0, 4 * unit_len, 0, False), (start, unit_len, 4 * unit_len, True)]
        )
        return carry

    lax.fori_loop(0, 4, branch, 0)

    def leaf(k, carry):
        start = pl.multiple_of((8 + k) * unit_len, unit_len)
        parent = pl.multiple_of((4 + k // 2) * unit_len, unit_len)
        one_unit(
            start,
            [
                (0, 4 * unit_len, 0, False),
                (parent, unit_len, 4 * unit_len, False),
                (start, unit_len, 5 * unit_len, True),
            ],
        )
        return carry

    lax.fori_loop(0, 8, leaf, 0)


def forward_kernel(
    pos_ref, slope_ref, x_ref, gain_ref, shift_ref, w_ref, qb_ref, ctx_ref, log_ref, hat_ref,
    normed_ref, q_s, k_s, v_s, vt_s, bias_s, c_s, *, heads, head_size
):
    width = heads * head_size
    unit_len = q_s.shape[0] // UNITS
    blocks, rows, model = x_ref.shape
    gain, shift = gain_ref[...], shift_ref[...]

    def one_pair(n, carry):
        values = x_ref[pl.ds(2 * n, 2)].reshape(2 * rows, model).astype(f32)
        hat, _ = normalize(values)
        normed = (hat * gain + shift).astype(bf16)
        hat_ref[pl.ds(2 * n, 2)] = hat.astype(bf16).reshape(2, rows, model)
        normed_ref[pl.ds(2 * n, 2)] = normed.reshape(2, rows, model)
        made = (nn_dot(normed, w_ref[...]) + qb_ref[...]).astype(bf16)
        for i in range(2):
            dst = pl.ds(pl.multiple_of(pos_ref[2 * n + i], rows), rows)
            for m, scratch in enumerate((q_s, k_s, v_s)):
                scratch[dst, :] = made[i * rows : (i + 1) * rows, m * width : (m + 1) * width]
        return carry

    lax.fori_loop(0, blocks // 2, one_pair, 0, unroll=2)
    fill_transposed(v_s, vt_s, unit_len)
    fill_bias(slope_ref, bias_s, heads, unit_len)
    scale = head_size ** (-0.5) * LOG2E
    columns = heads * unit_len
    key_row = lax.broadcasted_iota(jnp.int32, (unit_len, columns), 0)
    query_col = lax.broadcasted_iota(jnp.int32, (unit_len, columns), 1) % unit_len
    causal = key_row <= query_col

    def one_unit(start, pieces):
        stacked = head_stack(q_s[pl.ds(start, unit_len), :], heads, head_size)
        scores = []
        top = None
        for key_start, size, depth, diagonal in pieces:
            s = nt_dot(k_s[pl.ds(key_start, size), :], stacked) * scale
            s = s + bias_s[depth : depth + size, :]
            if diagonal:
                s = jnp.where(causal, s, masked_score)
            scores.append(s)
            m = jnp.max(s, axis=0, keepdims=True)
            top = m if top is None else jnp.maximum(top, m)
        total = None
        wide = None
        for (key_start, size, depth, diagonal), s in zip(pieces, scores):
            p = jnp.exp2(s - top)
            part = jnp.sum(p, axis=0, keepdims=True)
            total = part if total is None else total + part
            o = nn_dot(vt_s[:, pl.ds(key_start, size)], p.astype(bf16))
            wide = o if wide is None else wide + o
        wide = wide * (1.0 / total)
        log_ref[pl.ds(start // unit_len, 1), :] = top + jnp.log2(total)
        c_s[pl.ds(start, unit_len), :] = diag_of(wide, heads, head_size, unit_len).T.astype(bf16)

    over_units(unit_len, one_unit)
    for i in range(blocks):
        src = pl.ds(pl.multiple_of(pos_ref[i], rows), rows)
        ctx_ref[i, :, :] = c_s[src, :]


def backward_kernel(
    pos_ref, back_ref, slope_ref, q_s, k_s, v_s, log_ref, gctx_ref, hat_ref, wt_ref,
    out_ref, grad_ref, gain_ref, shift_ref,
    kt_s, g_s, bias_s, dq_s, dk_s, dv_s, *, heads, head_size
):
    width = heads * head_size
    unit_len = q_s.shape[0] // UNITS
    blocks, rows, model = hat_ref.shape
    for i in range(blocks):
        dst = pl.ds(pl.multiple_of(pos_ref[i], rows), rows)
        g_s[dst, :] = gctx_ref[i, :, :]
    fill_transposed(k_s, kt_s, unit_len)
    fill_bias(slope_ref, bias_s, heads, unit_len)
    dk_s[...] = jnp.zeros_like(dk_s)
    dv_s[...] = jnp.zeros_like(dv_s)
    size_scale = head_size ** (-0.5)
    scale = size_scale * LOG2E
    columns = heads * unit_len
    key_row = lax.broadcasted_iota(jnp.int32, (unit_len, columns), 0)
    query_col = lax.broadcasted_iota(jnp.int32, (unit_len, columns), 1) % unit_len
    causal = key_row <= query_col

    def one_unit(start, pieces):
        stacked = head_stack(q_s[pl.ds(start, unit_len), :], heads, head_size)
        grads = head_stack(g_s[pl.ds(start, unit_len), :], heads, head_size)
        log_total = log_ref[pl.ds(start // unit_len, 1), :]
        kept = []
        delta = None
        for key_start, size, depth, diagonal in pieces:
            s = nt_dot(k_s[pl.ds(key_start, size), :], stacked) * scale
            s = s + bias_s[depth : depth + size, :]
            if diagonal:
                s = jnp.where(causal, s, masked_score)
            p = jnp.exp2(s - log_total)
            gp = nt_dot(v_s[pl.ds(key_start, size), :], grads)
            kept.append((p, gp))
            part = jnp.sum(p * gp, axis=0, keepdims=True)
            delta = part if delta is None else delta + part
        wide = None
        for (key_start, size, depth, diagonal), (p, gp) in zip(pieces, kept):
            ds = (p * (gp - delta)).astype(bf16)
            keys = pl.ds(key_start, size)
            dv_s[keys, :] += nn_dot(p.astype(bf16), grads)
            dk_s[keys, :] += nn_dot(ds, stacked)
            o = nn_dot(kt_s[:, keys], ds)
            wide = o if wide is None else wide + o
        dq = diag_of(wide, heads, head_size, unit_len).T * size_scale
        dq_s[pl.ds(start, unit_len), :] = dq.astype(bf16)

    over_units(unit_len, one_unit)
    for i in range(blocks):
        src = pl.ds(pl.multiple_of(pos_ref[i], rows), rows)
        out_ref[i, :, :width] = dq_s[src, :]
        out_ref[i, :, width : 2 * width] = (dk_s[src, :] * size_scale).astype(bf16)
        out_ref[i, :, 2 * width :] = dv_s[src, :].astype(bf16)
    gain_ref[...] = jnp.zeros_like(gain_ref)
    shift_ref[...] = jnp.zeros_like(shift_ref)

    def one_pair(n, carry):
        first, second = back_ref[2 * n], back_ref[2 * n + 1]
        rows_in = jnp.concatenate([out_ref[first], out_ref[second]], axis=0)
        grad = nn_dot(rows_in, wt_ref[...])
        grad_ref[pl.ds(2 * n, 2)] = grad.astype(bf16).reshape(2, rows, model)
        hat = jnp.concatenate([hat_ref[first], hat_ref[second]], axis=0).astype(f32)
        gain_ref[...] += jnp.sum((grad * hat).reshape(-1, 8, model), axis=0)
        shift_ref[...] += jnp.sum(grad.reshape(-1, 8, model), axis=0)
        return carry

    lax.fori_loop(0, blocks // 2, one_pair, 0, unroll=2)


def attention_forward(pos, slopes, hidden, gain, shift, weight, bias, heads, head_size):
    blocks, rows, model = hidden.shape
    tokens, width = blocks * rows, heads * head_size
    unit_len = tokens // UNITS
    smem = pl.BlockSpec(memory_space=pltpu.SMEM)
    vmem = pl.BlockSpec(memory_space=pltpu.VMEM)
    seq = jax.ShapeDtypeStruct((tokens, width), bf16)
    return pl.pallas_call(
        lambda *refs: forward_kernel(*refs, heads=heads, head_size=head_size),
        out_shape=(
            jax.ShapeDtypeStruct((blocks, rows, width), bf16),
            jax.ShapeDtypeStruct((UNITS, heads * unit_len), f32),
            jax.ShapeDtypeStruct((blocks, rows, model), bf16),
            jax.ShapeDtypeStruct((blocks, rows, model), bf16),
            seq, seq, seq,
        ),
        in_specs=[smem, smem, vmem, vmem, vmem, vmem, vmem],
        out_specs=(vmem,) * 7,
        scratch_shapes=[
            pltpu.VMEM((width, tokens), bf16),
            pltpu.VMEM((6 * unit_len, heads * unit_len), f32), pltpu.VMEM((tokens, width), bf16),
        ],
        compiler_params=pltpu.CompilerParams(vmem_limit_bytes=40 * 2**20),
        cost_estimate=pl.CostEstimate(
            flops=tokens * tokens * width * 2 + 6 * tokens * model * width,
            bytes_accessed=tokens * model * 6, transcendentals=tokens * tokens * heads // 3,
        ),
    )(pos, slopes, hidden, gain[None], shift[None], weight, bias[None])


def attention_backward(pos, back, slopes, q, k, v, log_total, gctx, hat, weight_t, heads, head_size):
    blocks, rows, model = hat.shape
    tokens, width = blocks * rows, heads * head_size
    unit_len = tokens // UNITS
    smem = pl.BlockSpec(memory_space=pltpu.SMEM)
    vmem = pl.BlockSpec(memory_space=pltpu.VMEM)
    seq = lambda: pltpu.VMEM((tokens, width), bf16)
    acc = lambda: pltpu.VMEM((tokens, width), f32)
    return pl.pallas_call(
        lambda *refs: backward_kernel(*refs, heads=heads, head_size=head_size),
        out_shape=(
            jax.ShapeDtypeStruct((blocks, rows, 3 * width), bf16),
            jax.ShapeDtypeStruct((blocks, rows, model), bf16),
            jax.ShapeDtypeStruct((8, model), f32),
            jax.ShapeDtypeStruct((8, model), f32),
        ),
        in_specs=[smem, smem, smem] + [vmem] * 7,
        out_specs=(vmem,) * 4,
        scratch_shapes=[
            pltpu.VMEM((width, tokens), bf16), seq(),
            pltpu.VMEM((6 * unit_len, heads * unit_len), f32), seq(), acc(), acc(),
        ],
        compiler_params=pltpu.CompilerParams(vmem_limit_bytes=40 * 2**20),
        cost_estimate=pl.CostEstimate(
            flops=tokens * tokens * width * 5 + 6 * tokens * model * width,
            bytes_accessed=tokens * model * 6, transcendentals=tokens * tokens * heads // 3,
        ),
    )(pos, back, slopes, q, k, v, log_total, gctx, hat, weight_t)


def swap(values, axis, mask):
    size = lax.axis_size(axis)
    return lax.ppermute(values, axis, [(i, i ^ mask) for i in range(size)])


def masks_of(size):
    found, mask = [], 1
    while mask < size:
        found.append(mask)
        mask *= 2
    return found


def pick(values, dim, high):
    low, up = lax.index_in_dim(values, 0, dim, False), lax.index_in_dim(values, 1, dim, False)
    return jnp.where(high, up, low), jnp.where(high, low, up)


def grow(values, bits):
    for axis, mask, dim in bits:
        other = swap(values, axis, mask)
        high = (lax.axis_index(axis) & mask) != 0
        values = jnp.concatenate(
            [jnp.where(high, other, values), jnp.where(high, values, other)], axis=dim
        )
    return values


def shrink(values, bits):
    for axis, mask, dim in bits:
        keep, send = pick(values, dim, (lax.axis_index(axis) & mask) != 0)
        other = swap(send.astype(bf16), axis, mask)
        values = jnp.expand_dims(keep.astype(f32) + other.astype(f32), dim)
    return values


def scatter_blocks(partial, ranks):
    far = [m for m in masks_of(ranks) if m > 1]
    n = partial.shape[0] // 2
    other = swap(partial[n:].astype(bf16), "tok", 1)
    held = partial[:n].astype(f32) + other.astype(f32)
    done = []
    for half, masks in ((0, far), (1, far[::-1])):
        part = held[half * (n // 2) : (half + 1) * (n // 2)]
        for m in masks[::-1]:
            k = part.shape[0] // 2
            part = part[:k] + swap(part[k:].astype(bf16), "tok", m).astype(f32)
        done.append(part)
    return jnp.concatenate(done, axis=0)


def block_order(ranks):
    far = [m for m in masks_of(ranks) if m > 1]
    order = []
    for half, masks in ((0, far), (1, far[::-1])):
        seen = [0]
        for m in masks:
            seen = seen + [j ^ m for j in seen]
        order += [(j, half) for j in seen]
    return order + [(j ^ 1, half) for j, half in order]


MLP = 4


def gather_near(block):
    far = swap(block, "tok", 2)
    near = swap(block, "tok", 1)
    return jnp.stack([block, near, far, swap(far, "tok", 1)])


def scatter_near(partial):
    pairs = partial.reshape((2, 2) + partial.shape[1:])
    held = pairs[:, 0].astype(f32) + swap(pairs[:, 1].astype(bf16), "tok", 1).astype(f32)
    return held[0] + swap(held[1].astype(bf16), "tok", 2).astype(f32)


def on_device(
    hidden_in, output_cotangent, unit_place, ln1_gain, ln1_bias, qkv_weight, qv_bias, out_weight,
    out_bias, ln2_gain, ln2_bias, fc1_weight, fc1_bias, fc2_weight, fc2_bias,
):
    trees, rows, width = hidden_in.shape
    tok_size, leaf_size = lax.axis_size("tok"), lax.axis_size("leaf")
    ranks = tok_size // trees
    head_size = width // HEADS
    heads = HEADS // ranks
    lanes = heads * head_size
    hidden_units = fc1_weight.shape[1]
    own_units = fc1_bias.shape[0]
    weight_rows = qkv_weight.shape[0]
    groups = leaf_size * trees
    wide_groups = leaf_size * tok_size // MLP
    tokens = rows * tok_size
    unit_len = tokens // UNITS
    index = lax.axis_index("tok")
    tree, rank = index // ranks, index % ranks
    rank_groups = [[g * ranks + i for i in range(ranks)] for g in range(trees)]

    def exchange(values):
        mine = jnp.where(tree == 0, values[0], values[1])
        other = swap(jnp.where(tree == 0, values[1], values[0]), "tok", ranks)
        return jnp.stack([jnp.where(tree == 0, mine, other), jnp.where(tree == 0, other, mine)])

    mlp_groups = [[g * MLP + i for i in range(MLP)] for g in range(tok_size // MLP)]

    def to_ranks(values, among=rank_groups):
        return lax.all_to_all(values, "tok", 0, 0, tiled=True, axis_index_groups=among)

    leaf_bits = [("leaf", m) for m in masks_of(leaf_size)[::-1]]
    tok_bits = [("tok", m) for m in masks_of(tok_size)[::-1]]
    tree_bits = [b for b in tok_bits if b[1] >= ranks]
    high_bits = [b for b in tok_bits if b[1] >= MLP]
    narrow = [b + (d,) for d, b in enumerate(leaf_bits + tree_bits)]
    wide = [b + (d,) for d, b in enumerate(leaf_bits + high_bits)]
    leaves = len(leaf_bits)
    wide_leaf, wide_tok = wide[:leaves], wide[leaves:]
    route_a = wide_tok + wide_leaf
    route_b = wide_tok[:-1] + wide_leaf + wide_tok[-1:]

    def opened(values, bits):
        return values.reshape((1,) * len(bits) + values.shape)

    def split(values, bits):
        return values.reshape((2,) * len(bits) + values.shape[1:])

    def narrow_spread(values):
        return grow(opened(values, narrow), narrow[leaves:] + narrow[:leaves])

    def narrow_collect(values):
        done = shrink(split(values, narrow), narrow)
        return done.reshape(done.shape[len(narrow) :])

    order = block_order(ranks)
    half = jnp.arange(2 * ranks, dtype=jnp.int32) % 2
    peer = jnp.arange(2 * ranks, dtype=jnp.int32) // 2
    back = (rank ^ jnp.array([j for j, _ in order], jnp.int32)) * 2 + jnp.array(
        [h for _, h in order], jnp.int32
    )
    position = (half * ranks + peer) * rows
    place = jnp.where(tree == 0, unit_place[0], unit_place[1])
    slot = position // unit_len
    unit_at = jnp.sum(
        jnp.where(slot[:, None] == jnp.arange(UNITS, dtype=jnp.int32)[None, :], place[None, :], 0),
        axis=1,
    )
    pos = unit_at * unit_len + position % unit_len
    head_index = (rank * heads + jnp.arange(heads, dtype=jnp.int32)).astype(f32)
    slopes = jnp.exp2(-8.0 * (head_index + 1.0) / HEADS) * LOG2E

    hidden = exchange(hidden_in)
    hidden_all = lax.all_gather(
        hidden, "tok", axis=0, tiled=True, axis_index_groups=rank_groups
    )

    small = jnp.concatenate(
        [ln1_gain, ln1_bias, qv_bias, out_bias, ln2_gain, ln2_bias, fc1_bias, fc2_bias]
    )
    mixed_cols = 3 * lanes
    small_rows = -(-small.shape[0] // mixed_cols)
    small_block = jnp.pad(small, (0, small_rows * mixed_cols - small.shape[0]))
    small_block = jnp.broadcast_to(
        small_block.reshape(1, small_rows, mixed_cols), (ranks, small_rows, mixed_cols)
    )
    mixed_parts = (
        qkv_weight.reshape(weight_rows, 3, ranks, lanes)
        .transpose(2, 0, 1, 3)
        .reshape(ranks, weight_rows, mixed_cols)
    )
    up_cols = wide_groups * own_units
    up_parts = (
        fc1_weight.reshape(weight_rows, wide_groups, MLP, own_units)
        .transpose(2, 0, 1, 3)
        .reshape(MLP, weight_rows, up_cols)
    )
    mixed_sent = to_ranks(jnp.concatenate([mixed_parts, small_block], axis=1))
    mixed_all = narrow_spread(mixed_sent).reshape(
        groups, ranks, weight_rows + small_rows, mixed_cols
    )
    w_mixed = mixed_all[:, :, :weight_rows].reshape(width, mixed_cols)
    smalls = mixed_all[:, :, weight_rows:].reshape(groups * ranks, small_rows * mixed_cols)
    up_sent = to_ranks(up_parts, mlp_groups)
    up_weight = grow(opened(up_sent, wide), route_b).reshape(width, up_cols)
    down_weight = grow(opened(fc2_weight, wide), route_a).reshape(up_cols, width)
    out_rows = narrow_spread(out_weight).reshape(groups * weight_rows, width)
    w_output = (
        lax.all_gather(out_rows, "tok", axis=0, tiled=False, axis_index_groups=rank_groups)
        .reshape(ranks, groups, weight_rows, width)
        .transpose(1, 0, 2, 3)
        .reshape(width, width)
    )

    def small_of(start, array):
        n = array.shape[0]
        return smalls[:, start : start + n].reshape(-1).astype(f32), start + n

    gain_one, at = small_of(0, ln1_gain)
    shift_one, at = small_of(at, ln1_bias)
    bias_mixed, at = small_of(at, qv_bias)
    bias_output, at = small_of(at, out_bias)
    gain_two, at = small_of(at, ln2_gain)
    shift_two, at = small_of(at, ln2_bias)
    bias_up, at = small_of(at, fc1_bias)
    bias_down, at = small_of(at, fc2_bias)
    own_bias_up = lax.dynamic_index_in_dim(
        bias_up.reshape(wide_groups, MLP, own_units), index % MLP, 1, keepdims=False
    ).reshape(up_cols)
    query_bias = lax.dynamic_slice_in_dim(bias_mixed, rank * lanes, lanes)
    value_bias = lax.dynamic_slice_in_dim(bias_mixed, width + rank * lanes, lanes)

    cotangent = exchange(output_cotangent)
    cotangent_all = gather_near(cotangent.reshape(2 * rows, width))

    qkv_bias = jnp.concatenate([query_bias, jnp.zeros((lanes,), f32), value_bias])
    ctx_sent, log_total, hat_one, normed_one, queries, keys, values = attention_forward(
        pos, slopes, hidden_all, gain_one, shift_one, w_mixed, qkv_bias, heads, head_size
    )
    ctx_parts = to_ranks(ctx_sent.reshape(ranks, 2 * rows, lanes))
    context = ctx_parts.transpose(1, 0, 2).reshape(2, rows, width)

    branch_out = jnp.einsum("mrd,de->mre", context, w_output, preferred_element_type=f32)
    middle = hidden.astype(f32) + (branch_out + bias_output)
    hat_two, inverse_two = normalize(middle)
    normed_two = (hat_two * gain_two + shift_two).astype(bf16)
    normed_all = gather_near(normed_two.reshape(2 * rows, width))

    expand = jnp.einsum("brd,df->brf", normed_all, up_weight, preferred_element_type=f32)
    expand = expand + own_bias_up
    root = (2.0 / jnp.pi) ** 0.5
    square = expand * expand
    tanh = jnp.tanh(root * (expand + 0.044715 * square * expand))
    active = (0.5 * expand * (1.0 + tanh)).astype(bf16)
    slope = 0.5 * (1.0 + tanh) + 0.5 * expand * (1.0 - tanh * tanh) * root * (
        1.0 + 3 * 0.044715 * square
    )
    grad_active = jnp.einsum("brd,fd->brf", cotangent_all, down_weight, preferred_element_type=f32)
    grad_expand = (grad_active * slope).astype(bf16)
    grad_normed_part = jnp.einsum(
        "brf,df->brd", grad_expand, up_weight, preferred_element_type=f32
    ).astype(bf16)
    grad_normed_two = scatter_near(grad_normed_part).reshape(2, rows, width)

    reduced_part = jnp.einsum(
        "brf,fd->brd", active, down_weight, preferred_element_type=f32
    ).astype(bf16)
    reduced = scatter_near(reduced_part).reshape(2, rows, width)
    layer_out = exchange((middle + (reduced + bias_down)).astype(bf16))

    g_down = jnp.einsum("brf,brd->fd", active, cotangent_all, preferred_element_type=f32)
    g_up = jnp.einsum("brd,brf->df", normed_all, grad_expand, preferred_element_type=f32)
    g_bias_up = jnp.sum(grad_expand, axis=(0, 1), dtype=f32)
    g_down_own = shrink(
        split(g_down.reshape(wide_groups, own_units, width), wide), route_a[::-1]
    ).reshape(own_units, width)
    g_up_parts = shrink(
        split(g_up.reshape(wide_groups, MLP, weight_rows, up_cols), wide), route_b[::-1]
    ).reshape(MLP, weight_rows, up_cols)
    g_up_own = (
        to_ranks(g_up_parts.astype(bf16), mlp_groups)
        .reshape(MLP, weight_rows, wide_groups, own_units)
        .transpose(1, 2, 0, 3)
        .reshape(weight_rows, hidden_units)
        .astype(f32)
    )

    cot = cotangent.astype(f32)
    g_gain_two = jnp.sum(grad_normed_two * hat_two, axis=(0, 1))
    g_shift_two = jnp.sum(grad_normed_two, axis=(0, 1))
    g_bias_down = jnp.sum(cot, axis=(0, 1))
    grad_middle = cot + norm_back(hat_two, inverse_two, gain_two, grad_normed_two)
    grad_branch = grad_middle.astype(bf16)
    g_bias_output = jnp.sum(grad_branch, axis=(0, 1), dtype=f32)
    grad_context = jnp.einsum(
        "mre,de->mrd", grad_branch, w_output, preferred_element_type=f32
    ).astype(bf16)
    gctx_sent = grad_context.reshape(2 * rows, ranks, lanes).transpose(1, 0, 2)
    gctx_parts = to_ranks(gctx_sent).reshape(2 * ranks, rows, lanes)
    g_output = jnp.einsum("mrd,mre->de", context, grad_branch, preferred_element_type=f32)
    g_output_parts = (
        g_output.reshape(groups, ranks, weight_rows, width).transpose(1, 0, 2, 3).astype(bf16)
    )
    g_output_own = narrow_collect(
        lax.psum_scatter(
            g_output_parts.reshape(ranks * groups * weight_rows, width), "tok",
            scatter_dimension=0, tiled=True, axis_index_groups=rank_groups,
        ).reshape(groups, weight_rows, width)
    )

    grad_projected, grad_one_part, g_gain_part, g_shift_part = attention_backward(
        pos, back, slopes, queries, keys, values, log_total, gctx_parts, hat_one, w_mixed.T, heads,
        head_size,
    )
    g_gain_one = jnp.sum(g_gain_part, axis=0)
    g_shift_one = jnp.sum(g_shift_part, axis=0)
    grad_one = scatter_blocks(grad_one_part, ranks)
    hat_own, inverse_own = normalize(hidden.astype(f32))
    input_grad = exchange(
        (grad_middle + norm_back(hat_own, inverse_own, gain_one, grad_one)).astype(bf16)
    )

    g_mixed = jnp.einsum("brd,bre->de", normed_one, grad_projected, preferred_element_type=f32)
    g_bias_mixed = jnp.sum(grad_projected, axis=(0, 1), dtype=f32)
    own_lane = jnp.arange(ranks, dtype=jnp.int32)[:, None] == rank
    own_slice = jnp.arange(MLP, dtype=jnp.int32)[:, None] == index % MLP
    g_bias_query = jnp.where(own_lane, g_bias_mixed[None, :lanes], 0.0).reshape(-1)
    g_bias_value = jnp.where(own_lane, g_bias_mixed[None, 2 * lanes :], 0.0).reshape(-1)
    g_bias_up_all = jnp.where(
        own_slice[None], g_bias_up.reshape(wide_groups, 1, own_units), 0.0
    ).reshape(-1)
    pieces = [
        g_gain_one, g_shift_one, jnp.concatenate([g_bias_query, g_bias_value]), g_bias_output,
        g_gain_two, g_shift_two, g_bias_up_all, g_bias_down,
    ]
    sizes = [p.shape[0] // (groups * ranks) for p in pieces]
    g_small = jnp.concatenate([p.reshape(groups, ranks, -1) for p in pieces], axis=2)
    g_small = jnp.pad(g_small, ((0, 0), (0, 0), (0, small_rows * mixed_cols - g_small.shape[2])))
    g_sent = jnp.concatenate(
        [
            g_mixed.reshape(groups, ranks, weight_rows, mixed_cols),
            g_small.reshape(groups, ranks, small_rows, mixed_cols),
        ],
        axis=2,
    ).astype(bf16)
    g_back = to_ranks(narrow_collect(g_sent).astype(bf16))
    g_mixed_own = (
        g_back[:, :weight_rows]
        .reshape(ranks, weight_rows, 3, lanes)
        .transpose(1, 2, 0, 3)
        .reshape(weight_rows, 3 * width)
        .astype(f32)
    )
    small_sum = jnp.sum(g_back[:, weight_rows:].astype(f32), axis=0).reshape(-1)
    found, at = [], 0
    for size in sizes:
        found.append(small_sum[at : at + size])
        at += size
    (
        o_gain_one, o_shift_one, o_bias_mixed, o_bias_output, o_gain_two, o_shift_two, o_bias_up,
        o_bias_down,
    ) = found
    return (
        layer_out, input_grad, o_gain_one, o_shift_one, g_mixed_own, o_bias_mixed, g_output_own,
        o_bias_output, o_gain_two, o_shift_two, g_up_own, o_bias_up, g_down_own, o_bias_down,
    )


def solution(mesh):
    both = ("leaf", "tok")
    tokens, matrix, vector = P("leaf", "tok", None), P(both, None), P(both)
    return jax.shard_map(
        on_device,
        mesh=mesh,
        in_specs=(
            tokens, tokens, P("leaf", None), vector, vector, matrix, vector, matrix, vector, vector,
            vector, matrix, vector, matrix, vector,
        ),
        out_specs=(
            tokens, tokens, vector, vector, matrix, vector, matrix, vector, vector, vector, matrix,
            vector, matrix, vector,
        ),
        check_vma=False,
    )
```

```python
import jax
import jax.numpy as jnp
from jax import lax
from jax.experimental import pallas as pl
from jax.experimental.pallas import tpu as pltpu
from jax.sharding import PartitionSpec as P

HEADS = 16
UNITS = 16
LOG2E = 1.4426950408889634
WAITS = {
    "down_o0": "xa",
    "down_v0": "mixed",
    "output_back_o0": "held",
    "up_o1": "xa",
}


def tie(value, name, **there):
    key = WAITS.get(name)
    return after(value, there[key]) if key else value


layer_eps = 1e-05
masked_score = -1e30
f32 = jnp.float32
bf16 = jnp.bfloat16


def normalize(values):
    row_mean = jnp.mean(values, axis=-1, keepdims=True)
    centered = values - row_mean
    spread = jnp.mean(centered * centered, axis=-1, keepdims=True)
    inverse = lax.rsqrt(spread + layer_eps)
    return centered * inverse, inverse


def norm_back(hat, inverse, gain, grad):
    scaled = grad * gain
    first = jnp.mean(scaled, axis=-1, keepdims=True)
    second = jnp.mean(scaled * hat, axis=-1, keepdims=True)
    return (scaled - first - hat * second) * inverse


def fill_transposed(src, dst, unit_len):
    for u in range(UNITS):
        dst[:, u * unit_len : (u + 1) * unit_len] = (
            src[u * unit_len : (u + 1) * unit_len, :].astype(f32).T.astype(bf16)
        )


def head_stack(block, heads, head_size):
    if heads == 1:
        return block
    lane = lax.broadcasted_iota(jnp.int32, block.shape, 1) // head_size
    return jnp.concatenate(
        [jnp.where(lane == h, block, jnp.zeros_like(block)) for h in range(heads)], axis=0
    )


def fill_bias(slope_ref, bias_ref, heads, unit_len):
    depth = lax.broadcasted_iota(jnp.int32, (bias_ref.shape[0], unit_len), 0).astype(f32)
    for h in range(heads):
        bias_ref[:, h * unit_len : (h + 1) * unit_len] = depth * slope_ref[h]


def nt_dot(left, right):
    return lax.dot_general(left, right, (((1,), (1,)), ((), ())), preferred_element_type=f32)


def nn_dot(left, right):
    return lax.dot_general(left, right, (((1,), (0,)), ((), ())), preferred_element_type=f32)


def diag_of(wide, heads, head_size, unit_len):
    return jnp.concatenate(
        [
            wide[h * head_size : (h + 1) * head_size, h * unit_len : (h + 1) * unit_len]
            for h in range(heads)
        ],
        axis=0,
    )


def over_units(unit_len, one_unit):
    for u in range(4):
        pieces = [(u * unit_len, unit_len, u * unit_len, True)]
        if u:
            pieces = [(0, u * unit_len, 0, False)] + pieces
        one_unit(u * unit_len, pieces)

    def branch(b, carry):
        start = pl.multiple_of((4 + b) * unit_len, unit_len)
        one_unit(
            start, [(0, 4 * unit_len, 0, False), (start, unit_len, 4 * unit_len, True)]
        )
        return carry

    lax.fori_loop(0, 4, branch, 0)

    def leaf(k, carry):
        start = pl.multiple_of((8 + k) * unit_len, unit_len)
        parent = pl.multiple_of((4 + k // 2) * unit_len, unit_len)
        one_unit(
            start,
            [
                (0, 4 * unit_len, 0, False),
                (parent, unit_len, 4 * unit_len, False),
                (start, unit_len, 5 * unit_len, True),
            ],
        )
        return carry

    lax.fori_loop(0, 8, leaf, 0)


def forward_kernel(
    pos_ref, slope_ref, x_ref, gain_ref, shift_ref, w_ref, qb_ref, ctx_ref, log_ref, hat_out,
    normed_out, qkv_out, hat_s, normed_s, qkv_s, vt_s, bias_s, c_s, sems, *, heads, head_size
):
    width = heads * head_size
    blocks, rows, model = x_ref.shape
    unit_len = blocks * rows // UNITS
    gain, shift = gain_ref[...], shift_ref[...]
    q_s, k_s, v_s = qkv_s.at[0], qkv_s.at[1], qkv_s.at[2]

    def out_copies(n):
        part = pl.ds(2 * n, 2)
        return (
            pltpu.make_async_copy(hat_s.at[part], hat_out.at[part], sems.at[0, n]),
            pltpu.make_async_copy(normed_s.at[part], normed_out.at[part], sems.at[1, n]),
        )

    for n in range(blocks // 2):
        values = x_ref[2 * n : 2 * n + 2].reshape(2 * rows, model).astype(f32)
        hat, _ = normalize(values)
        normed = (hat * gain + shift).astype(bf16)
        hat_s[2 * n : 2 * n + 2] = hat.astype(bf16).reshape(2, rows, model)
        normed_s[2 * n : 2 * n + 2] = normed.reshape(2, rows, model)
        for copy in out_copies(n):
            copy.start()
        made = (nn_dot(normed, w_ref[...]) + qb_ref[...]).astype(bf16)
        for i in range(2):
            dst = pl.ds(pl.multiple_of(pos_ref[2 * n + i], rows), rows)
            for m in range(3):
                qkv_s[m, dst, :] = made[i * rows : (i + 1) * rows, m * width : (m + 1) * width]
    qkv_copy = pltpu.make_async_copy(qkv_s, qkv_out, sems.at[2, 0])
    qkv_copy.start()
    fill_transposed(v_s, vt_s, unit_len)
    fill_bias(slope_ref, bias_s, heads, unit_len)
    scale = head_size ** (-0.5) * LOG2E
    columns = heads * unit_len
    key_row = lax.broadcasted_iota(jnp.int32, (unit_len, columns), 0)
    query_col = lax.broadcasted_iota(jnp.int32, (unit_len, columns), 1) % unit_len
    causal = key_row <= query_col

    def one_unit(start, pieces):
        stacked = head_stack(q_s[pl.ds(start, unit_len), :], heads, head_size)
        scores = []
        top = None
        for key_start, size, depth, diagonal in pieces:
            s = nt_dot(k_s[pl.ds(key_start, size), :], stacked) * scale
            s = s + bias_s[depth : depth + size, :]
            if diagonal:
                s = jnp.where(causal, s, masked_score)
            scores.append(s)
            m = jnp.max(s, axis=0, keepdims=True)
            top = m if top is None else jnp.maximum(top, m)
        total = None
        wide = None
        for (key_start, size, depth, diagonal), s in zip(pieces, scores):
            p = jnp.exp2(s - top)
            part = jnp.sum(p, axis=0, keepdims=True)
            total = part if total is None else total + part
            o = nn_dot(vt_s[:, pl.ds(key_start, size)], p.astype(bf16))
            wide = o if wide is None else wide + o
        wide = wide * (1.0 / total)
        log_ref[pl.ds(start // unit_len, 1), :] = top + jnp.log2(total)
        c_s[pl.ds(start, unit_len), :] = diag_of(wide, heads, head_size, unit_len).T.astype(bf16)

    over_units(unit_len, one_unit)
    for i in range(blocks):
        src = pl.ds(pl.multiple_of(pos_ref[i], rows), rows)
        ctx_ref[i, :, :] = c_s[src, :]
    for n in range(blocks // 2):
        for copy in out_copies(n):
            copy.wait()
    qkv_copy.wait()


def project_back(back_ref, first_block, out_ref, hat_ref, wt_ref, grad_ref, gain_ref, shift_ref):
    count, rows, model = grad_ref.shape
    gain_ref[...] = jnp.zeros_like(gain_ref)
    shift_ref[...] = jnp.zeros_like(shift_ref)
    for n in range(0, count, 2):
        first, second = back_ref[first_block + n], back_ref[first_block + n + 1]
        rows_in = jnp.concatenate([out_ref[first], out_ref[second]], axis=0)
        grad = nn_dot(rows_in, wt_ref[...])
        grad_ref[n : n + 2] = grad.astype(bf16).reshape(2, rows, model)
        hat = jnp.concatenate([hat_ref[first], hat_ref[second]], axis=0).astype(f32)
        gain_ref[...] += jnp.sum((grad * hat).reshape(-1, 8, model), axis=0)
        shift_ref[...] += jnp.sum(grad.reshape(-1, 8, model), axis=0)


def project_kernel(back_ref, out_ref, hat_ref, wt_ref, grad_ref, gain_ref, shift_ref):
    project_back(back_ref, 0, out_ref, hat_ref, wt_ref, grad_ref, gain_ref, shift_ref)


def backward_kernel(
    pos_ref, back_ref, slope_ref, qkv_in, log_ref, gctx_ref, hat_in, wt_ref,
    out_ref, grad_ref, gain_ref, shift_ref,
    qkv_s, hat_s, kt_s, g_s, bias_s, dq_s, dk_s, dv_s, sems, *, heads, head_size
):
    width = heads * head_size
    blocks, rows, model = hat_in.shape
    unit_len = blocks * rows // UNITS
    qkv_copy = pltpu.make_async_copy(qkv_in, qkv_s, sems.at[0])
    qkv_copy.start()
    hat_copy = pltpu.make_async_copy(hat_in, hat_s, sems.at[1])
    hat_copy.start()
    q_s, k_s, v_s = qkv_s.at[0], qkv_s.at[1], qkv_s.at[2]
    for i in range(blocks):
        dst = pl.ds(pl.multiple_of(pos_ref[i], rows), rows)
        g_s[dst, :] = gctx_ref[i, :, :]
    qkv_copy.wait()
    fill_transposed(k_s, kt_s, unit_len)
    fill_bias(slope_ref, bias_s, heads, unit_len)
    dk_s[...] = jnp.zeros_like(dk_s)
    dv_s[...] = jnp.zeros_like(dv_s)
    size_scale = head_size ** (-0.5)
    scale = size_scale * LOG2E
    columns = heads * unit_len
    key_row = lax.broadcasted_iota(jnp.int32, (unit_len, columns), 0)
    query_col = lax.broadcasted_iota(jnp.int32, (unit_len, columns), 1) % unit_len
    causal = key_row <= query_col

    def one_unit(start, pieces):
        stacked = head_stack(q_s[pl.ds(start, unit_len), :], heads, head_size)
        grads = head_stack(g_s[pl.ds(start, unit_len), :], heads, head_size)
        log_total = log_ref[pl.ds(start // unit_len, 1), :]
        kept = []
        delta = None
        for key_start, size, depth, diagonal in pieces:
            s = nt_dot(k_s[pl.ds(key_start, size), :], stacked) * scale
            s = s + bias_s[depth : depth + size, :]
            if diagonal:
                s = jnp.where(causal, s, masked_score)
            p = jnp.exp2(s - log_total)
            gp = nt_dot(v_s[pl.ds(key_start, size), :], grads)
            kept.append((p, gp))
            part = jnp.sum(p * gp, axis=0, keepdims=True)
            delta = part if delta is None else delta + part
        wide = None
        for (key_start, size, depth, diagonal), (p, gp) in zip(pieces, kept):
            ds = (p * (gp - delta)).astype(bf16)
            keys = pl.ds(key_start, size)
            dv_s[keys, :] += nn_dot(p.astype(bf16), grads)
            dk_s[keys, :] += nn_dot(ds, stacked)
            o = nn_dot(kt_s[:, keys], ds)
            wide = o if wide is None else wide + o
        dq = diag_of(wide, heads, head_size, unit_len).T * size_scale
        dq_s[pl.ds(start, unit_len), :] = dq.astype(bf16)

    over_units(unit_len, one_unit)
    for i in range(blocks):
        src = pl.ds(pl.multiple_of(pos_ref[i], rows), rows)
        out_ref[i, :, :width] = dq_s[src, :]
        out_ref[i, :, width : 2 * width] = (dk_s[src, :] * size_scale).astype(bf16)
        out_ref[i, :, 2 * width :] = dv_s[src, :].astype(bf16)
    hat_copy.wait()
    project_back(back_ref, blocks // 2, out_ref, hat_s, wt_ref, grad_ref, gain_ref, shift_ref)


def memory_specs(count, kind):
    return [pl.BlockSpec(memory_space=kind)] * count


def attention_forward(pos, slopes, hidden, gain, shift, weight, bias, heads, head_size):
    blocks, rows, model = hidden.shape
    tokens, width = blocks * rows, heads * head_size
    unit_len = tokens // UNITS
    whole = jax.ShapeDtypeStruct((blocks, rows, model), bf16)
    return pl.pallas_call(
        lambda *refs: forward_kernel(*refs, heads=heads, head_size=head_size),
        out_shape=(
            jax.ShapeDtypeStruct((blocks, rows, width), bf16),
            jax.ShapeDtypeStruct((UNITS, heads * unit_len), f32),
            whole, whole, jax.ShapeDtypeStruct((3, tokens, width), bf16),
        ),
        in_specs=memory_specs(2, pltpu.SMEM) + memory_specs(5, pltpu.VMEM),
        out_specs=tuple(memory_specs(2, pltpu.VMEM) + memory_specs(3, pltpu.HBM)),
        scratch_shapes=[
            pltpu.VMEM((blocks, rows, model), bf16), pltpu.VMEM((blocks, rows, model), bf16),
            pltpu.VMEM((3, tokens, width), bf16), pltpu.VMEM((width, tokens), bf16),
            pltpu.VMEM((6 * unit_len, heads * unit_len), f32), pltpu.VMEM((tokens, width), bf16),
            pltpu.SemaphoreType.DMA((3, blocks // 2)),
        ],
        compiler_params=pltpu.CompilerParams(vmem_limit_bytes=60 * 2**20),
        cost_estimate=pl.CostEstimate(
            flops=2000000000, bytes_accessed=2**20, transcendentals=0,
        ),
    )(pos, slopes, hidden, gain[None], shift[None], weight, bias[None])


def attention_backward(
    pos, back, slopes, qkv, log_total, gctx, hat, weight_t, heads, head_size
):
    blocks, rows, model = hat.shape
    tokens, width = blocks * rows, heads * head_size
    unit_len = tokens // UNITS
    seq = lambda: pltpu.VMEM((tokens, width), bf16)
    acc = lambda: pltpu.VMEM((tokens, width), f32)
    hbm, vmem = memory_specs(1, pltpu.HBM), memory_specs(1, pltpu.VMEM)
    return pl.pallas_call(
        lambda *refs: backward_kernel(*refs, heads=heads, head_size=head_size),
        out_shape=(
            jax.ShapeDtypeStruct((blocks, rows, 3 * width), bf16),
            jax.ShapeDtypeStruct((blocks // 2, rows, model), bf16),
            jax.ShapeDtypeStruct((8, model), f32),
            jax.ShapeDtypeStruct((8, model), f32),
        ),
        in_specs=memory_specs(3, pltpu.SMEM) + hbm + vmem * 2 + hbm + vmem,
        out_specs=tuple(vmem * 4),
        scratch_shapes=[
            pltpu.VMEM((3, tokens, width), bf16), pltpu.VMEM((blocks, rows, model), bf16),
            pltpu.VMEM((width, tokens), bf16), seq(),
            pltpu.VMEM((6 * unit_len, heads * unit_len), f32), seq(), acc(), acc(),
            pltpu.SemaphoreType.DMA((2,)),
        ],
        compiler_params=pltpu.CompilerParams(vmem_limit_bytes=48 * 2**20),
        cost_estimate=pl.CostEstimate(
            flops=2000000000, bytes_accessed=2**20, transcendentals=0,
        ),
    )(pos, back, slopes, qkv, log_total, gctx, hat, weight_t)


def project_own(back, grad_projected, hat, weight_t):
    blocks, rows, model = hat.shape
    return pl.pallas_call(
        project_kernel,
        out_shape=(
            jax.ShapeDtypeStruct((blocks // 2, rows, model), bf16),
            jax.ShapeDtypeStruct((8, model), f32),
            jax.ShapeDtypeStruct((8, model), f32),
        ),
        in_specs=memory_specs(1, pltpu.SMEM) + memory_specs(3, pltpu.VMEM),
        out_specs=tuple(memory_specs(3, pltpu.VMEM)),
        compiler_params=pltpu.CompilerParams(vmem_limit_bytes=24 * 2**20),
        cost_estimate=pl.CostEstimate(
            flops=2000000000, bytes_accessed=2**20, transcendentals=0,
        ),
    )(back, grad_projected, hat, weight_t)


def call(body, outs, inputs, scratch=(), smem=0, limit=60, hbm_out=()):
    specs = memory_specs(smem, pltpu.SMEM) + memory_specs(len(inputs) - smem, pltpu.VMEM)
    return pl.pallas_call(
        body,
        out_shape=tuple(outs),
        in_specs=specs,
        out_specs=tuple(memory_specs(len(outs), pltpu.VMEM)),
        scratch_shapes=list(scratch),
        compiler_params=pltpu.CompilerParams(vmem_limit_bytes=limit * 2**20),
        cost_estimate=pl.CostEstimate(flops=2**20, bytes_accessed=2**20, transcendentals=0),
    )(*inputs)


def shaped(shape, kind=bf16):
    return jax.ShapeDtypeStruct(shape, kind)


def tn_dot(left, right):
    return lax.dot_general(left, right, (((0,), (0,)), ((), ())), preferred_element_type=f32)


def mixed_kernel(normed_ref, grad_ref, out_ref, sum_ref):
    blocks, rows, width = normed_ref.shape
    grads = grad_ref[...].reshape(blocks * rows, -1)
    sum_ref[...] = jnp.sum(grads.astype(f32).reshape(-1, 8, grads.shape[1]), axis=0)
    for i in range(0, width, 256):
        part = tn_dot(normed_ref[:, :, i : i + 256].reshape(blocks * rows, 256), grads)
        out_ref[i : i + 256, :] = part.astype(bf16)


def mixed_gradient(normed, grads):
    return call(
        mixed_kernel,
        (shaped((normed.shape[2], grads.shape[2])), shaped((8, grads.shape[2]), f32)),
        (normed, grads), limit=24,
    )


def swap(values, axis, mask):
    size = lax.axis_size(axis)
    return lax.ppermute(values, axis, [(i, i ^ mask) for i in range(size)])


def masks_of(size):
    found, mask = [], 1
    while mask < size:
        found.append(mask)
        mask *= 2
    return found


def pick(values, dim, high):
    low, up = lax.index_in_dim(values, 0, dim, False), lax.index_in_dim(values, 1, dim, False)
    return jnp.where(high, up, low), jnp.where(high, low, up)


def grow(values, bits, name="", **there):
    for n, (axis, mask, dim) in enumerate(bits):
        values = tie(values, name + f"v{n}", **there)
        other = tie(swap(values, axis, mask), name + f"o{n}", **there)
        high = (lax.axis_index(axis) & mask) != 0
        values = jnp.concatenate(
            [jnp.where(high, other, values), jnp.where(high, values, other)], axis=dim
        )
    return values


def shrink(values, bits, name="", **there):
    for n, (axis, mask, dim) in enumerate(bits):
        values = tie(values, name + f"v{n}", **there)
        keep, send = pick(values, dim, (lax.axis_index(axis) & mask) != 0)
        other = tie(swap(send.astype(bf16), axis, mask), name + f"o{n}", **there)
        values = jnp.expand_dims((keep.astype(f32) + other.astype(f32)).astype(bf16), dim)
    return values


def routes(ranks):
    far = [m for m in masks_of(ranks) if m > 1]
    return far[::-1], far


def block_order(ranks):
    order = []
    for half, masks in enumerate(routes(ranks)):
        seen = [0]
        for m in masks:
            seen = seen + [j ^ m for j in seen]
        order += [(j, half) for j in seen]
    return order + [(j ^ 1, half) for j, half in order]


def after(value, *needed):
    return lax.optimization_barrier((value,) + needed)[0]


MLP = 4


def gather_near(block):
    far = swap(block, "tok", 2)
    near = swap(block, "tok", 1)
    return [block, near, far, swap(far, "tok", 1)]


def scatter_near(partial):
    pairs = partial.reshape((2, 2) + partial.shape[1:])
    held = pairs[:, 0].astype(f32) + swap(pairs[:, 1].astype(bf16), "tok", 1).astype(f32)
    return held[0] + swap(held[1].astype(bf16), "tok", 2).astype(f32)


def on_device(
    hidden_in, output_cotangent, unit_place, ln1_gain, ln1_bias, qkv_weight, qv_bias, out_weight,
    out_bias, ln2_gain, ln2_bias, fc1_weight, fc1_bias, fc2_weight, fc2_bias,
):
    trees, rows, width = hidden_in.shape
    tok_size, leaf_size = lax.axis_size("tok"), lax.axis_size("leaf")
    ranks = tok_size // trees
    head_size = width // HEADS
    heads = HEADS // ranks
    lanes = heads * head_size
    hidden_units = fc1_weight.shape[1]
    own_units = fc1_bias.shape[0]
    weight_rows = qkv_weight.shape[0]
    groups = leaf_size * trees
    wide_groups = leaf_size * tok_size // MLP
    tokens = rows * tok_size
    unit_len = tokens // UNITS
    index = lax.axis_index("tok")
    tree, rank = index // ranks, index % ranks
    rank_groups = [[g * ranks + i for i in range(ranks)] for g in range(trees)]

    def trade(values):
        own = jnp.where(tree == 0, values[0], values[1])
        return own, swap(jnp.where(tree == 0, values[1], values[0]), "tok", ranks)

    def trade_back(own, away):
        other = swap(away, "tok", ranks)
        return jnp.stack([jnp.where(tree == 0, own, other), jnp.where(tree == 0, other, own)])

    mlp_groups = [[g * MLP + i for i in range(MLP)] for g in range(tok_size // MLP)]

    def to_ranks(values, among=rank_groups):
        return lax.all_to_all(values, "tok", 0, 0, tiled=True, axis_index_groups=among)

    leaf_bits = [("leaf", m) for m in masks_of(leaf_size)[::-1]]
    tok_bits = [("tok", m) for m in masks_of(tok_size)[::-1]]
    tree_bits = [b for b in tok_bits if b[1] >= ranks]
    high_bits = [b for b in tok_bits if b[1] >= MLP]
    narrow = [b + (d,) for d, b in enumerate(leaf_bits + tree_bits)]
    wide = [b + (d,) for d, b in enumerate(leaf_bits + high_bits)]
    leaves = len(leaf_bits)
    wide_leaf, wide_tok = wide[:leaves], wide[leaves:]
    route_a = wide_tok + wide_leaf
    route_b = wide_tok[:-1] + wide_leaf + wide_tok[-1:]

    def opened(values, bits):
        return values.reshape((1,) * len(bits) + values.shape)

    def split(values, bits):
        return values.reshape((2,) * len(bits) + values.shape[1:])

    half = tree ^ (jnp.arange(2 * ranks, dtype=jnp.int32) % 2)
    peer = jnp.arange(2 * ranks, dtype=jnp.int32) // 2
    order = block_order(ranks)
    back = (rank ^ jnp.array([j for j, _ in order], jnp.int32)) * 2 + jnp.array(
        [h for _, h in order], jnp.int32
    )
    position = (half * ranks + peer) * rows
    place = jnp.where(tree == 0, unit_place[0], unit_place[1])
    slot = position // unit_len
    unit_at = jnp.sum(
        jnp.where(slot[:, None] == jnp.arange(UNITS, dtype=jnp.int32)[None, :], place[None, :], 0),
        axis=1,
    )
    pos = unit_at * unit_len + position % unit_len
    head_index = (rank * heads + jnp.arange(heads, dtype=jnp.int32)).astype(f32)
    slopes = jnp.exp2(-8.0 * (head_index + 1.0) / HEADS) * LOG2E

    vectors = [ln1_gain, ln1_bias, qv_bias, out_bias, ln2_gain, ln2_bias, fc1_bias, fc2_bias]
    small_size = sum(v.shape[0] for v in vectors)
    mixed_cols = 3 * lanes
    small_rows = -(-small_size // mixed_cols)
    small_block, at = jnp.zeros((small_rows * mixed_cols,), bf16), 0
    for v in vectors:
        small_block += jnp.pad(v, (at, small_rows * mixed_cols - at - v.shape[0]))
        at += v.shape[0]
    small_block = jnp.broadcast_to(
        small_block.reshape(1, small_rows, mixed_cols), (ranks, small_rows, mixed_cols)
    )
    mixed_parts = (
        qkv_weight.reshape(weight_rows, 3, ranks, lanes)
        .transpose(2, 0, 1, 3)
        .reshape(ranks, weight_rows, mixed_cols)
    )
    up_cols = wide_groups * own_units
    up_parts = (
        fc1_weight.reshape(weight_rows, wide_groups, MLP, own_units)
        .transpose(2, 0, 1, 3)
        .reshape(MLP, weight_rows, up_cols)
    )
    mixed_sent = to_ranks(jnp.concatenate([mixed_parts, small_block], axis=1))
    hidden = tie(jnp.stack(trade(hidden_in)), "input", mixed=mixed_sent)
    hidden_all = lax.all_gather(
        hidden, "tok", axis=0, tiled=True, axis_index_groups=rank_groups
    )
    mixed_all = grow(opened(mixed_sent, narrow), narrow[leaves:] + narrow[:leaves]).reshape(
        groups, ranks, weight_rows + small_rows, mixed_cols
    )
    w_mixed = mixed_all[:, :, :weight_rows].reshape(width, mixed_cols)
    smalls = mixed_all[:, :, weight_rows:].reshape(groups * ranks, small_rows * mixed_cols)
    up_sent = to_ranks(tie(up_parts, "up", mixed=mixed_sent, all=mixed_all, x=hidden), mlp_groups)
    out_rows = grow(
        opened(tie(out_weight, "output", mixed=mixed_sent, all=mixed_all, x=hidden), narrow),
        narrow[leaves:] + narrow[:leaves],
    ).reshape(groups * weight_rows, width)
    w_output = (
        lax.all_gather(tie(out_rows, "output_gather", all=mixed_all, x=hidden_all), "tok", axis=0, tiled=False, axis_index_groups=rank_groups)
        .reshape(ranks, groups, weight_rows, width)
        .transpose(1, 0, 2, 3)
        .reshape(width, width)
    )

    def small_of(start, array):
        n = array.shape[0]
        return smalls[:, start : start + n].reshape(-1).astype(f32), start + n

    gain_one, at = small_of(0, ln1_gain)
    shift_one, at = small_of(at, ln1_bias)
    bias_mixed, at = small_of(at, qv_bias)
    bias_output, at = small_of(at, out_bias)
    gain_two, at = small_of(at, ln2_gain)
    shift_two, at = small_of(at, ln2_bias)
    bias_up, at = small_of(at, fc1_bias)
    bias_down, at = small_of(at, fc2_bias)
    own_bias_up = lax.dynamic_index_in_dim(
        bias_up.reshape(wide_groups, MLP, own_units), index % MLP, 1, keepdims=False
    ).reshape(up_cols)
    query_bias = lax.dynamic_slice_in_dim(bias_mixed, rank * lanes, lanes)
    value_bias = lax.dynamic_slice_in_dim(bias_mixed, width + rank * lanes, lanes)

    cotangent = jnp.stack(trade(tie(output_cotangent, "cotangent", mixed=mixed_sent, all=mixed_all, x=hidden)))

    qkv_bias = jnp.concatenate([query_bias, jnp.zeros((lanes,), f32), value_bias])
    ctx_sent, log_total, hat_one, normed_one, qkv = attention_forward(
        pos, slopes, hidden_all, gain_one, shift_one, w_mixed, qkv_bias, heads, head_size
    )
    ctx_parts = to_ranks(ctx_sent.reshape(ranks, 2 * rows, lanes))
    context = ctx_parts.transpose(1, 0, 2).reshape(2, rows, width)
    there = dict(mixed=mixed_sent, all=mixed_all, x=hidden, xa=hidden_all, ctx=ctx_sent, parts=ctx_parts)
    kinds = (
        list(range(len(leaf_bits))), list(range(len(leaf_bits), len(wide) - 1)), [len(wide) - 1]
    )

    def ordered(kind_order):
        return [wide[i] for kind in kind_order for i in kinds[kind]]

    order_up, order_down = ordered((1, 0, 2)), ordered((1, 2, 0))
    up_weight = grow(opened(up_sent, wide), order_up, "up_", **there).reshape(width, up_cols)
    down_weight = grow(opened(fc2_weight, wide), order_down, "down_", **there).reshape(up_cols, width)
    cotangent_all = gather_near(tie(cotangent, "near", **there).reshape(2 * rows, width))
    branch_out = jnp.einsum("mrd,de->mre", context, w_output, preferred_element_type=f32)
    middle = hidden.astype(f32) + (branch_out + bias_output)
    hat_two, inverse_two = normalize(middle)
    normed_two = (hat_two * gain_two + shift_two).astype(bf16)
    normed_all = gather_near(normed_two.reshape(2 * rows, width))

    normed_all, cotangent_all = jnp.stack(normed_all), jnp.stack(cotangent_all)
    expand = jnp.einsum("brd,df->brf", normed_all, up_weight, preferred_element_type=f32)
    expand = expand + own_bias_up
    root = (2.0 / jnp.pi) ** 0.5
    square = expand * expand
    tanh = jnp.tanh(root * (expand + 0.044715 * square * expand))
    active = (0.5 * expand * (1.0 + tanh)).astype(bf16)
    slope = 0.5 * (1.0 + tanh) + 0.5 * expand * (1.0 - tanh * tanh) * root * (
        1.0 + 3 * 0.044715 * square
    )
    grad_active = jnp.einsum("brd,fd->brf", cotangent_all, down_weight, preferred_element_type=f32)
    grad_expand = (grad_active * slope).astype(bf16)
    grad_normed_part = jnp.einsum(
        "brf,df->brd", grad_expand, up_weight, preferred_element_type=f32
    ).astype(bf16)
    grad_normed_two = scatter_near(grad_normed_part)
    g_bias_up = jnp.sum(grad_expand, axis=(0, 1), dtype=f32)
    grad_first = grad_normed_part
    grad_normed_two = grad_normed_two.reshape(2, rows, width)

    reduced_part = jnp.einsum(
        "brf,fd->brd", tie(active, "reduced", g=grad_normed_two, p=grad_first), down_weight, preferred_element_type=f32
    ).astype(bf16)
    reduced = scatter_near(tie(reduced_part, "reduced_sent", g=grad_normed_two)).reshape(2, rows, width)
    g_down = jnp.einsum(
        "brf,brd->fd", tie(active, "down_made", g=grad_normed_two, p=grad_first), cotangent_all, preferred_element_type=f32
    ).astype(bf16)
    g_up = jnp.einsum(
        "brd,brf->df", normed_all, tie(grad_expand, "up_made", g=grad_normed_two, p=grad_first), preferred_element_type=f32
    ).astype(bf16)
    cot = cotangent.astype(f32)
    g_gain_two = jnp.sum(grad_normed_two * hat_two, axis=(0, 1))
    g_shift_two = jnp.sum(grad_normed_two, axis=(0, 1))
    g_bias_down = jnp.sum(cot, axis=(0, 1))
    grad_middle = cot + norm_back(hat_two, inverse_two, gain_two, grad_normed_two)
    grad_branch = grad_middle.astype(bf16)
    g_bias_output = jnp.sum(grad_branch, axis=(0, 1), dtype=f32)
    grad_context = jnp.einsum(
        "mre,de->mrd", grad_branch, w_output, preferred_element_type=f32
    ).astype(bf16)
    gctx_sent = grad_context.reshape(2 * rows, ranks, lanes).transpose(1, 0, 2)
    gctx_parts = to_ranks(gctx_sent).reshape(2 * ranks, rows, lanes)
    g_output = jnp.einsum("mrd,mre->de", context, grad_branch, preferred_element_type=f32)

    weight_t = w_mixed.T
    grad_projected, grad_sent, g_gain_far, g_shift_far = attention_backward(
        pos, back, slopes, qkv, log_total, gctx_parts, hat_one, weight_t, heads, head_size
    )
    grad_kept, g_gain_near, g_shift_near = project_own(back, grad_projected, hat_one, weight_t)
    g_gain_one = jnp.sum(g_gain_far + g_gain_near, axis=0)
    g_shift_one = jnp.sum(g_shift_far + g_shift_near, axis=0)
    held = (grad_kept.astype(f32) + swap(grad_sent, "tok", 1).astype(f32)).astype(bf16)
    pieces = [held[: held.shape[0] // 2], held[held.shape[0] // 2 :]]
    steps = [held]
    passes = list(zip(*[route[::-1] for route in routes(ranks)]))
    for m_own, m_other in passes:
        kind = f32 if pieces[0].shape[0] == 2 else bf16
        k = pieces[0].shape[0] // 2
        pieces = [
            (piece[:k].astype(f32) + swap(piece[k:].astype(bf16), "tok", m).astype(f32)).astype(kind)
            for piece, m in zip(pieces, (m_own, m_other))
        ]
        steps.append(pieces[1])
    grad_one = jnp.concatenate(pieces, axis=0)
    hat_own, inverse_own = normalize(hidden.astype(f32))
    input_half = (grad_middle + norm_back(hat_own, inverse_own, gain_one, grad_one)).astype(bf16)
    input_grad = trade_back(input_half[0], input_half[1])

    there = dict(
        g=grad_normed_two, gc=grad_context, gp=gctx_parts, ke=grad_sent, held=steps[0], s2=steps[1], s3=steps[-1],
    )
    back_down, back_up = ordered((0, 2, 1)), ordered((2, 0, 1))
    finished = (middle + (reduced + bias_down)).astype(bf16)
    layer_out = trade_back(finished[0], tie(finished[1], "layer_out", **there))
    g_down_own = shrink(
        split(g_down.reshape(wide_groups, own_units, width), wide), back_down, "down_back_", **there
    ).reshape(own_units, width).astype(f32)
    g_up_parts = shrink(
        split(g_up.reshape(wide_groups, MLP, weight_rows, up_cols), wide), back_up, "up_back_", **there
    ).reshape(MLP, weight_rows, up_cols)
    g_up_own = (
        to_ranks(tie(g_up_parts.astype(bf16), "up_back", **there), mlp_groups)
        .reshape(MLP, weight_rows, wide_groups, own_units)
        .transpose(1, 2, 0, 3)
        .reshape(weight_rows, hidden_units)
        .astype(f32)
    )
    g_output_parts = (
        tie(g_output, "output_sum", **there)
        .reshape(groups, ranks, weight_rows, width)
        .transpose(1, 0, 2, 3)
        .astype(bf16)
        .reshape(ranks * groups * weight_rows, width)
    )
    g_output_group = lax.psum_scatter(
        g_output_parts, "tok", scatter_dimension=0, tiled=True, axis_index_groups=rank_groups
    )
    g_output_own = shrink(
        split(tie(g_output_group, "output_own", **there).reshape(groups, weight_rows, width), narrow), narrow, "output_back_", **there
    ).reshape(weight_rows, width).astype(f32)

    mixed_from = tie(grad_projected, "mixed_made", **there)
    g_mixed, g_bias_mixed = mixed_gradient(normed_one, mixed_from)
    g_bias_mixed = jnp.sum(g_bias_mixed, axis=0)
    own_lane = jnp.arange(ranks, dtype=jnp.int32)[:, None] == rank
    own_slice = jnp.arange(MLP, dtype=jnp.int32)[:, None] == index % MLP
    g_bias_query = jnp.where(own_lane, g_bias_mixed[None, :lanes], 0.0).reshape(-1)
    g_bias_value = jnp.where(own_lane, g_bias_mixed[None, 2 * lanes :], 0.0).reshape(-1)
    g_bias_up_all = jnp.where(
        own_slice[None], g_bias_up.reshape(wide_groups, 1, own_units), 0.0
    ).reshape(-1)
    pieces = [
        g_gain_one, g_shift_one, jnp.concatenate([g_bias_query, g_bias_value]), g_bias_output,
        g_gain_two, g_shift_two, g_bias_up_all, g_bias_down,
    ]
    sizes = [p.shape[0] // (groups * ranks) for p in pieces]
    g_small = jnp.concatenate([p.reshape(groups, ranks, -1) for p in pieces], axis=2)
    g_small = jnp.pad(g_small, ((0, 0), (0, 0), (0, small_rows * mixed_cols - g_small.shape[2])))
    g_sent = jnp.concatenate(
        [
            g_mixed.reshape(groups, ranks, weight_rows, mixed_cols),
            g_small.reshape(groups, ranks, small_rows, mixed_cols),
        ],
        axis=2,
    ).astype(bf16)
    g_held = shrink(split(g_sent, narrow), narrow, "mixed_back_", **there)
    g_back = to_ranks(
        tie(g_held.astype(bf16), "mixed_back", **there).reshape(
            ranks, weight_rows + small_rows, mixed_cols
        )
    )
    g_mixed_own = (
        g_back[:, :weight_rows]
        .reshape(ranks, weight_rows, 3, lanes)
        .transpose(1, 2, 0, 3)
        .reshape(weight_rows, 3 * width)
        .astype(f32)
    )
    small_sum = jnp.sum(g_back[:, weight_rows:].astype(f32), axis=0).reshape(-1)
    found, at = [], 0
    for size in sizes:
        found.append(small_sum[at : at + size])
        at += size
    (
        o_gain_one, o_shift_one, o_bias_mixed, o_bias_output, o_gain_two, o_shift_two, o_bias_up,
        o_bias_down,
    ) = found
    return (
        layer_out, input_grad, o_gain_one, o_shift_one, g_mixed_own, o_bias_mixed, g_output_own,
        o_bias_output, o_gain_two, o_shift_two, g_up_own, o_bias_up, g_down_own, o_bias_down,
    )


def solution(mesh):
    both = ("leaf", "tok")
    tokens, matrix, vector = P("leaf", "tok", None), P(both, None), P(both)
    return jax.shard_map(
        on_device,
        mesh=mesh,
        in_specs=(
            tokens, tokens, P("leaf", None), vector, vector, matrix, vector, matrix, vector, vector,
            vector, matrix, vector, matrix, vector,
        ),
        out_specs=(
            tokens, tokens, vector, vector, matrix, vector, matrix, vector, vector, vector, matrix,
            vector, matrix, vector,
        ),
        check_vma=False,
    )
```

```python
import jax
import jax.numpy as jnp
from jax import lax
from jax.experimental import pallas as pl
from jax.experimental.pallas import tpu as pltpu
from jax.sharding import PartitionSpec as P

HEADS = 16
UNITS = 16
LOG2E = 1.4426950408889634
WAITS = {
    "down_o0": "xa",
    "down_v0": "mixed",
    "output_back_o0": "held",
    "up_o1": "xa",
}


def tie(value, name, **there):
    key = WAITS.get(name)
    return after(value, there[key]) if key else value


layer_eps = 1e-05
masked_score = -1e30
f32 = jnp.float32
bf16 = jnp.bfloat16


def normalize(values):
    row_mean = jnp.mean(values, axis=-1, keepdims=True)
    centered = values - row_mean
    spread = jnp.mean(centered * centered, axis=-1, keepdims=True)
    inverse = lax.rsqrt(spread + layer_eps)
    return centered * inverse, inverse


def norm_back(hat, inverse, gain, grad):
    scaled = grad * gain
    first = jnp.mean(scaled, axis=-1, keepdims=True)
    second = jnp.mean(scaled * hat, axis=-1, keepdims=True)
    return (scaled - first - hat * second) * inverse


def fill_transposed(src, dst, unit_len):
    for u in range(UNITS):
        dst[:, u * unit_len : (u + 1) * unit_len] = (
            src[u * unit_len : (u + 1) * unit_len, :].astype(f32).T.astype(bf16)
        )


def head_stack(block, heads, head_size):
    if heads == 1:
        return block
    lane = lax.broadcasted_iota(jnp.int32, block.shape, 1) // head_size
    return jnp.concatenate(
        [jnp.where(lane == h, block, jnp.zeros_like(block)) for h in range(heads)], axis=0
    )


def fill_bias(slope_ref, bias_ref, heads, unit_len):
    depth = lax.broadcasted_iota(jnp.int32, (bias_ref.shape[0], unit_len), 0).astype(f32)
    for h in range(heads):
        bias_ref[:, h * unit_len : (h + 1) * unit_len] = depth * slope_ref[h]


def nt_dot(left, right):
    return lax.dot_general(left, right, (((1,), (1,)), ((), ())), preferred_element_type=f32)


def nn_dot(left, right):
    return lax.dot_general(left, right, (((1,), (0,)), ((), ())), preferred_element_type=f32)


def diag_of(wide, heads, head_size, unit_len):
    return jnp.concatenate(
        [
            wide[h * head_size : (h + 1) * head_size, h * unit_len : (h + 1) * unit_len]
            for h in range(heads)
        ],
        axis=0,
    )


def over_units(unit_len, one_unit):
    for u in range(4):
        pieces = [(u * unit_len, unit_len, u * unit_len, True)]
        if u:
            pieces = [(0, u * unit_len, 0, False)] + pieces
        one_unit(u * unit_len, pieces)

    def branch(b, carry):
        start = pl.multiple_of((4 + b) * unit_len, unit_len)
        one_unit(
            start, [(0, 4 * unit_len, 0, False), (start, unit_len, 4 * unit_len, True)]
        )
        return carry

    lax.fori_loop(0, 4, branch, 0, unroll=4)

    def leaf(k, carry):
        start = pl.multiple_of((8 + k) * unit_len, unit_len)
        parent = pl.multiple_of((4 + k // 2) * unit_len, unit_len)
        one_unit(
            start,
            [
                (0, 4 * unit_len, 0, False),
                (parent, unit_len, 4 * unit_len, False),
                (start, unit_len, 5 * unit_len, True),
            ],
        )
        return carry

    lax.fori_loop(0, 8, leaf, 0, unroll=4)


def forward_kernel(
    pos_ref, slope_ref, x_ref, gain_ref, shift_ref, w_ref, qb_ref, ctx_ref, log_ref, hat_out,
    normed_out, qkv_out, hat_s, normed_s, qkv_s, vt_s, bias_s, c_s, sems, *, heads, head_size
):
    width = heads * head_size
    blocks, rows, model = x_ref.shape
    unit_len = blocks * rows // UNITS
    gain, shift = gain_ref[...], shift_ref[...]
    q_s, k_s, v_s = qkv_s.at[0], qkv_s.at[1], qkv_s.at[2]

    def out_copies(n):
        part = pl.ds(2 * n, 2)
        return (
            pltpu.make_async_copy(hat_s.at[part], hat_out.at[part], sems.at[0, n]),
            pltpu.make_async_copy(normed_s.at[part], normed_out.at[part], sems.at[1, n]),
        )

    for n in range(blocks // 2):
        values = x_ref[2 * n : 2 * n + 2].reshape(2 * rows, model).astype(f32)
        hat, _ = normalize(values)
        normed = (hat * gain + shift).astype(bf16)
        hat_s[2 * n : 2 * n + 2] = hat.astype(bf16).reshape(2, rows, model)
        normed_s[2 * n : 2 * n + 2] = normed.reshape(2, rows, model)
        for copy in out_copies(n):
            copy.start()
        made = (nn_dot(normed, w_ref[...]) + qb_ref[...]).astype(bf16)
        for i in range(2):
            dst = pl.ds(pl.multiple_of(pos_ref[2 * n + i], rows), rows)
            for m in range(3):
                qkv_s[m, dst, :] = made[i * rows : (i + 1) * rows, m * width : (m + 1) * width]
    qkv_copy = pltpu.make_async_copy(qkv_s, qkv_out, sems.at[2, 0])
    qkv_copy.start()
    fill_transposed(v_s, vt_s, unit_len)
    fill_bias(slope_ref, bias_s, heads, unit_len)
    scale = head_size ** (-0.5) * LOG2E
    columns = heads * unit_len
    key_row = lax.broadcasted_iota(jnp.int32, (unit_len, columns), 0)
    query_col = lax.broadcasted_iota(jnp.int32, (unit_len, columns), 1) % unit_len
    causal = key_row <= query_col

    def one_unit(start, pieces):
        stacked = head_stack(q_s[pl.ds(start, unit_len), :], heads, head_size)
        scores = []
        top = None
        for key_start, size, depth, diagonal in pieces:
            s = nt_dot(k_s[pl.ds(key_start, size), :], stacked) * scale
            s = s + bias_s[depth : depth + size, :]
            if diagonal:
                s = jnp.where(causal, s, masked_score)
            scores.append(s)
            m = jnp.max(s, axis=0, keepdims=True)
            top = m if top is None else jnp.maximum(top, m)
        total = None
        wide = None
        for (key_start, size, depth, diagonal), s in zip(pieces, scores):
            p = jnp.exp2(s - top)
            part = jnp.sum(p, axis=0, keepdims=True)
            total = part if total is None else total + part
            o = nn_dot(vt_s[:, pl.ds(key_start, size)], p.astype(bf16))
            wide = o if wide is None else wide + o
        wide = wide * (1.0 / total)
        log_ref[pl.ds(start // unit_len, 1), :] = top + jnp.log2(total)
        c_s[pl.ds(start, unit_len), :] = diag_of(wide, heads, head_size, unit_len).T.astype(bf16)

    over_units(unit_len, one_unit)
    for i in range(blocks):
        src = pl.ds(pl.multiple_of(pos_ref[i], rows), rows)
        ctx_ref[i, :, :] = c_s[src, :]
    for n in range(blocks // 2):
        for copy in out_copies(n):
            copy.wait()
    qkv_copy.wait()


def project_back(back_ref, first_block, out_ref, hat_ref, wt_ref, grad_ref, gain_ref, shift_ref):
    count, rows, model = grad_ref.shape
    gain_ref[...] = jnp.zeros_like(gain_ref)
    shift_ref[...] = jnp.zeros_like(shift_ref)
    for n in range(0, count, 2):
        first, second = back_ref[first_block + n], back_ref[first_block + n + 1]
        rows_in = jnp.concatenate([out_ref[first], out_ref[second]], axis=0)
        grad = nn_dot(rows_in, wt_ref[...])
        grad_ref[n : n + 2] = grad.astype(bf16).reshape(2, rows, model)
        hat = jnp.concatenate([hat_ref[first], hat_ref[second]], axis=0).astype(f32)
        gain_ref[...] += jnp.sum((grad * hat).reshape(-1, 8, model), axis=0)
        shift_ref[...] += jnp.sum(grad.reshape(-1, 8, model), axis=0)


def project_kernel(back_ref, out_ref, hat_ref, wt_ref, grad_ref, gain_ref, shift_ref):
    project_back(back_ref, 0, out_ref, hat_ref, wt_ref, grad_ref, gain_ref, shift_ref)


def backward_kernel(
    pos_ref, back_ref, slope_ref, qkv_in, log_ref, gctx_ref, hat_in, wt_ref,
    out_ref, grad_ref, gain_ref, shift_ref,
    qkv_s, hat_s, kt_s, g_s, bias_s, dq_s, dk_s, dv_s, sems, *, heads, head_size
):
    width = heads * head_size
    blocks, rows, model = hat_in.shape
    unit_len = blocks * rows // UNITS
    qkv_copy = pltpu.make_async_copy(qkv_in, qkv_s, sems.at[0])
    qkv_copy.start()
    hat_copy = pltpu.make_async_copy(hat_in, hat_s, sems.at[1])
    hat_copy.start()
    q_s, k_s, v_s = qkv_s.at[0], qkv_s.at[1], qkv_s.at[2]
    for i in range(blocks):
        dst = pl.ds(pl.multiple_of(pos_ref[i], rows), rows)
        g_s[dst, :] = gctx_ref[i, :, :]
    qkv_copy.wait()
    fill_transposed(k_s, kt_s, unit_len)
    fill_bias(slope_ref, bias_s, heads, unit_len)
    dk_s[...] = jnp.zeros_like(dk_s)
    dv_s[...] = jnp.zeros_like(dv_s)
    size_scale = head_size ** (-0.5)
    scale = size_scale * LOG2E
    columns = heads * unit_len
    key_row = lax.broadcasted_iota(jnp.int32, (unit_len, columns), 0)
    query_col = lax.broadcasted_iota(jnp.int32, (unit_len, columns), 1) % unit_len
    causal = key_row <= query_col

    def one_unit(start, pieces):
        stacked = head_stack(q_s[pl.ds(start, unit_len), :], heads, head_size)
        grads = head_stack(g_s[pl.ds(start, unit_len), :], heads, head_size)
        log_total = log_ref[pl.ds(start // unit_len, 1), :]
        kept = []
        delta = None
        for key_start, size, depth, diagonal in pieces:
            s = nt_dot(k_s[pl.ds(key_start, size), :], stacked) * scale
            s = s + bias_s[depth : depth + size, :]
            if diagonal:
                s = jnp.where(causal, s, masked_score)
            p = jnp.exp2(s - log_total)
            gp = nt_dot(v_s[pl.ds(key_start, size), :], grads)
            kept.append((p, gp))
            part = jnp.sum(p * gp, axis=0, keepdims=True)
            delta = part if delta is None else delta + part
        wide = None
        for (key_start, size, depth, diagonal), (p, gp) in zip(pieces, kept):
            ds = (p * (gp - delta)).astype(bf16)
            keys = pl.ds(key_start, size)
            dv_s[keys, :] += nn_dot(p.astype(bf16), grads)
            dk_s[keys, :] += nn_dot(ds, stacked)
            o = nn_dot(kt_s[:, keys], ds)
            wide = o if wide is None else wide + o
        dq = diag_of(wide, heads, head_size, unit_len).T * size_scale
        dq_s[pl.ds(start, unit_len), :] = dq.astype(bf16)

    over_units(unit_len, one_unit)
    for i in range(blocks):
        src = pl.ds(pl.multiple_of(pos_ref[i], rows), rows)
        out_ref[i, :, :width] = dq_s[src, :]
        out_ref[i, :, width : 2 * width] = (dk_s[src, :] * size_scale).astype(bf16)
        out_ref[i, :, 2 * width :] = dv_s[src, :].astype(bf16)
    hat_copy.wait()
    project_back(back_ref, blocks // 2, out_ref, hat_s, wt_ref, grad_ref, gain_ref, shift_ref)


def memory_specs(count, kind):
    return [pl.BlockSpec(memory_space=kind)] * count


def attention_forward(pos, slopes, hidden, gain, shift, weight, bias, heads, head_size):
    blocks, rows, model = hidden.shape
    tokens, width = blocks * rows, heads * head_size
    unit_len = tokens // UNITS
    whole = jax.ShapeDtypeStruct((blocks, rows, model), bf16)
    return pl.pallas_call(
        lambda *refs: forward_kernel(*refs, heads=heads, head_size=head_size),
        out_shape=(
            jax.ShapeDtypeStruct((blocks, rows, width), bf16),
            jax.ShapeDtypeStruct((UNITS, heads * unit_len), f32),
            whole, whole, jax.ShapeDtypeStruct((3, tokens, width), bf16),
        ),
        in_specs=memory_specs(2, pltpu.SMEM) + memory_specs(5, pltpu.VMEM),
        out_specs=tuple(memory_specs(2, pltpu.VMEM) + memory_specs(3, pltpu.HBM)),
        scratch_shapes=[
            pltpu.VMEM((blocks, rows, model), bf16), pltpu.VMEM((blocks, rows, model), bf16),
            pltpu.VMEM((3, tokens, width), bf16), pltpu.VMEM((width, tokens), bf16),
            pltpu.VMEM((6 * unit_len, heads * unit_len), f32), pltpu.VMEM((tokens, width), bf16),
            pltpu.SemaphoreType.DMA((3, blocks // 2)),
        ],
        compiler_params=pltpu.CompilerParams(vmem_limit_bytes=60 * 2**20),
        cost_estimate=pl.CostEstimate(
            flops=2000000000, bytes_accessed=2**20, transcendentals=0,
        ),
    )(pos, slopes, hidden, gain[None], shift[None], weight, bias[None])


def attention_backward(
    pos, back, slopes, qkv, log_total, gctx, hat, weight_t, heads, head_size
):
    blocks, rows, model = hat.shape
    tokens, width = blocks * rows, heads * head_size
    unit_len = tokens // UNITS
    seq = lambda: pltpu.VMEM((tokens, width), bf16)
    acc = lambda: pltpu.VMEM((tokens, width), f32)
    hbm, vmem = memory_specs(1, pltpu.HBM), memory_specs(1, pltpu.VMEM)
    return pl.pallas_call(
        lambda *refs: backward_kernel(*refs, heads=heads, head_size=head_size),
        out_shape=(
            jax.ShapeDtypeStruct((blocks, rows, 3 * width), bf16),
            jax.ShapeDtypeStruct((blocks // 2, rows, model), bf16),
            jax.ShapeDtypeStruct((8, model), f32),
            jax.ShapeDtypeStruct((8, model), f32),
        ),
        in_specs=memory_specs(3, pltpu.SMEM) + hbm + vmem * 2 + hbm + vmem,
        out_specs=tuple(vmem * 4),
        scratch_shapes=[
            pltpu.VMEM((3, tokens, width), bf16), pltpu.VMEM((blocks, rows, model), bf16),
            pltpu.VMEM((width, tokens), bf16), seq(),
            pltpu.VMEM((6 * unit_len, heads * unit_len), f32), seq(), acc(), acc(),
            pltpu.SemaphoreType.DMA((2,)),
        ],
        compiler_params=pltpu.CompilerParams(vmem_limit_bytes=48 * 2**20),
        cost_estimate=pl.CostEstimate(
            flops=2000000000, bytes_accessed=2**20, transcendentals=0,
        ),
    )(pos, back, slopes, qkv, log_total, gctx, hat, weight_t)


def project_own(back, grad_projected, hat, weight_t):
    blocks, rows, model = hat.shape
    return pl.pallas_call(
        project_kernel,
        out_shape=(
            jax.ShapeDtypeStruct((blocks // 2, rows, model), bf16),
            jax.ShapeDtypeStruct((8, model), f32),
            jax.ShapeDtypeStruct((8, model), f32),
        ),
        in_specs=memory_specs(1, pltpu.SMEM) + memory_specs(3, pltpu.VMEM),
        out_specs=tuple(memory_specs(3, pltpu.VMEM)),
        compiler_params=pltpu.CompilerParams(vmem_limit_bytes=24 * 2**20),
        cost_estimate=pl.CostEstimate(
            flops=2000000000, bytes_accessed=2**20, transcendentals=0,
        ),
    )(back, grad_projected, hat, weight_t)


def call(body, outs, inputs, scratch=(), smem=0, limit=60, hbm_out=()):
    specs = memory_specs(smem, pltpu.SMEM) + memory_specs(len(inputs) - smem, pltpu.VMEM)
    return pl.pallas_call(
        body,
        out_shape=tuple(outs),
        in_specs=specs,
        out_specs=tuple(memory_specs(len(outs), pltpu.VMEM)),
        scratch_shapes=list(scratch),
        compiler_params=pltpu.CompilerParams(vmem_limit_bytes=limit * 2**20),
        cost_estimate=pl.CostEstimate(flops=2**20, bytes_accessed=2**20, transcendentals=0),
    )(*inputs)


def shaped(shape, kind=bf16):
    return jax.ShapeDtypeStruct(shape, kind)


def tn_dot(left, right):
    return lax.dot_general(left, right, (((0,), (0,)), ((), ())), preferred_element_type=f32)


def mixed_kernel(normed_ref, grad_ref, out_ref, sum_ref):
    blocks, rows, width = normed_ref.shape
    grads = grad_ref[...].reshape(blocks * rows, -1)
    sum_ref[...] = jnp.sum(grads.astype(f32).reshape(-1, 8, grads.shape[1]), axis=0)
    for i in range(0, width, 256):
        part = tn_dot(normed_ref[:, :, i : i + 256].reshape(blocks * rows, 256), grads)
        out_ref[i : i + 256, :] = part.astype(bf16)


def mixed_gradient(normed, grads):
    return call(
        mixed_kernel,
        (shaped((normed.shape[2], grads.shape[2])), shaped((8, grads.shape[2]), f32)),
        (normed, grads), limit=24,
    )


def swap(values, axis, mask):
    size = lax.axis_size(axis)
    return lax.ppermute(values, axis, [(i, i ^ mask) for i in range(size)])


def masks_of(size):
    found, mask = [], 1
    while mask < size:
        found.append(mask)
        mask *= 2
    return found


def pick(values, dim, high):
    low, up = lax.index_in_dim(values, 0, dim, False), lax.index_in_dim(values, 1, dim, False)
    return jnp.where(high, up, low), jnp.where(high, low, up)


def grow(values, bits, name="", **there):
    for n, (axis, mask, dim) in enumerate(bits):
        values = tie(values, name + f"v{n}", **there)
        other = tie(swap(values, axis, mask), name + f"o{n}", **there)
        high = (lax.axis_index(axis) & mask) != 0
        values = jnp.concatenate(
            [jnp.where(high, other, values), jnp.where(high, values, other)], axis=dim
        )
    return values


def shrink(values, bits, name="", **there):
    for n, (axis, mask, dim) in enumerate(bits):
        values = tie(values, name + f"v{n}", **there)
        keep, send = pick(values, dim, (lax.axis_index(axis) & mask) != 0)
        other = tie(swap(send.astype(bf16), axis, mask), name + f"o{n}", **there)
        values = jnp.expand_dims((keep.astype(f32) + other.astype(f32)).astype(bf16), dim)
    return values


def routes(ranks):
    far = [m for m in masks_of(ranks) if m > 1]
    return far[::-1], far


def block_order(ranks):
    order = []
    for half, masks in enumerate(routes(ranks)):
        seen = [0]
        for m in masks:
            seen = seen + [j ^ m for j in seen]
        order += [(j, half) for j in seen]
    return order + [(j ^ 1, half) for j, half in order]


def after(value, *needed):
    return lax.optimization_barrier((value,) + needed)[0]


MLP = 4


def gather_near(block):
    far = swap(block, "tok", 2)
    near = swap(block, "tok", 1)
    return [block, near, far, swap(far, "tok", 1)]


def scatter_near(partial):
    pairs = partial.reshape((2, 2) + partial.shape[1:])
    held = pairs[:, 0].astype(f32) + swap(pairs[:, 1].astype(bf16), "tok", 1).astype(f32)
    return held[0] + swap(held[1].astype(bf16), "tok", 2).astype(f32)


def on_device(
    hidden_in, output_cotangent, unit_place, ln1_gain, ln1_bias, qkv_weight, qv_bias, out_weight,
    out_bias, ln2_gain, ln2_bias, fc1_weight, fc1_bias, fc2_weight, fc2_bias,
):
    trees, rows, width = hidden_in.shape
    tok_size, leaf_size = lax.axis_size("tok"), lax.axis_size("leaf")
    ranks = tok_size // trees
    head_size = width // HEADS
    heads = HEADS // ranks
    lanes = heads * head_size
    hidden_units = fc1_weight.shape[1]
    own_units = fc1_bias.shape[0]
    weight_rows = qkv_weight.shape[0]
    groups = leaf_size * trees
    wide_groups = leaf_size * tok_size // MLP
    tokens = rows * tok_size
    unit_len = tokens // UNITS
    index = lax.axis_index("tok")
    tree, rank = index // ranks, index % ranks
    rank_groups = [[g * ranks + i for i in range(ranks)] for g in range(trees)]

    def trade(values):
        own = jnp.where(tree == 0, values[0], values[1])
        return own, swap(jnp.where(tree == 0, values[1], values[0]), "tok", ranks)

    def trade_back(own, away):
        other = swap(away, "tok", ranks)
        return jnp.stack([jnp.where(tree == 0, own, other), jnp.where(tree == 0, other, own)])

    mlp_groups = [[g * MLP + i for i in range(MLP)] for g in range(tok_size // MLP)]

    def to_ranks(values, among=rank_groups):
        return lax.all_to_all(values, "tok", 0, 0, tiled=True, axis_index_groups=among)

    leaf_bits = [("leaf", m) for m in masks_of(leaf_size)[::-1]]
    tok_bits = [("tok", m) for m in masks_of(tok_size)[::-1]]
    tree_bits = [b for b in tok_bits if b[1] >= ranks]
    high_bits = [b for b in tok_bits if b[1] >= MLP]
    narrow = [b + (d,) for d, b in enumerate(leaf_bits + tree_bits)]
    wide = [b + (d,) for d, b in enumerate(leaf_bits + high_bits)]
    leaves = len(leaf_bits)
    wide_leaf, wide_tok = wide[:leaves], wide[leaves:]
    route_a = wide_tok + wide_leaf
    route_b = wide_tok[:-1] + wide_leaf + wide_tok[-1:]

    def turned(leaf_first):
        return list(narrow) if leaf_first else narrow[leaves:] + narrow[:leaves]

    def opened(values, bits):
        return values.reshape((1,) * len(bits) + values.shape)

    def split(values, bits):
        return values.reshape((2,) * len(bits) + values.shape[1:])

    half = tree ^ (jnp.arange(2 * ranks, dtype=jnp.int32) % 2)
    peer = jnp.arange(2 * ranks, dtype=jnp.int32) // 2
    order = block_order(ranks)
    back = (rank ^ jnp.array([j for j, _ in order], jnp.int32)) * 2 + jnp.array(
        [h for _, h in order], jnp.int32
    )
    position = (half * ranks + peer) * rows
    place = jnp.where(tree == 0, unit_place[0], unit_place[1])
    slot = position // unit_len
    unit_at = jnp.sum(
        jnp.where(slot[:, None] == jnp.arange(UNITS, dtype=jnp.int32)[None, :], place[None, :], 0),
        axis=1,
    )
    pos = unit_at * unit_len + position % unit_len
    head_index = (rank * heads + jnp.arange(heads, dtype=jnp.int32)).astype(f32)
    slopes = jnp.exp2(-8.0 * (head_index + 1.0) / HEADS) * LOG2E

    vectors = [ln1_gain, ln1_bias, qv_bias, out_bias, ln2_gain, ln2_bias, fc1_bias, fc2_bias]
    small_size = sum(v.shape[0] for v in vectors)
    mixed_cols = 3 * lanes
    small_rows = -(-small_size // mixed_cols)
    small_block, at = jnp.zeros((small_rows * mixed_cols,), bf16), 0
    for v in vectors:
        small_block += jnp.pad(v, (at, small_rows * mixed_cols - at - v.shape[0]))
        at += v.shape[0]
    small_block = jnp.broadcast_to(
        small_block.reshape(1, small_rows, mixed_cols), (ranks, small_rows, mixed_cols)
    )
    mixed_parts = (
        qkv_weight.reshape(weight_rows, 3, ranks, lanes)
        .transpose(2, 0, 1, 3)
        .reshape(ranks, weight_rows, mixed_cols)
    )
    up_cols = wide_groups * own_units
    up_parts = (
        fc1_weight.reshape(weight_rows, wide_groups, MLP, own_units)
        .transpose(2, 0, 1, 3)
        .reshape(MLP, weight_rows, up_cols)
    )
    mixed_sent = to_ranks(jnp.concatenate([mixed_parts, small_block], axis=1))
    hidden = tie(jnp.stack(trade(hidden_in)), "input", mixed=mixed_sent)
    hidden_all = lax.all_gather(
        hidden, "tok", axis=0, tiled=True, axis_index_groups=rank_groups
    )
    mixed_all = grow(opened(mixed_sent, narrow), turned(False)).reshape(
        groups, ranks, weight_rows + small_rows, mixed_cols
    )
    w_mixed = mixed_all[:, :, :weight_rows].reshape(width, mixed_cols)
    smalls = mixed_all[:, :, weight_rows:].reshape(groups * ranks, small_rows * mixed_cols)
    up_sent = to_ranks(tie(up_parts, "up", mixed=mixed_sent, all=mixed_all, x=hidden), mlp_groups)
    out_rows = grow(
        opened(tie(out_weight, "output", mixed=mixed_sent, all=mixed_all, x=hidden), narrow),
        turned(False),
    ).reshape(groups * weight_rows, width)
    w_output = (
        lax.all_gather(tie(out_rows, "output_gather", all=mixed_all, x=hidden_all), "tok", axis=0, tiled=False, axis_index_groups=rank_groups)
        .reshape(ranks, groups, weight_rows, width)
        .transpose(1, 0, 2, 3)
        .reshape(width, width)
    )

    def small_of(start, array):
        n = array.shape[0]
        return smalls[:, start : start + n].reshape(-1).astype(f32), start + n

    gain_one, at = small_of(0, ln1_gain)
    shift_one, at = small_of(at, ln1_bias)
    bias_mixed, at = small_of(at, qv_bias)
    bias_output, at = small_of(at, out_bias)
    gain_two, at = small_of(at, ln2_gain)
    shift_two, at = small_of(at, ln2_bias)
    bias_up, at = small_of(at, fc1_bias)
    bias_down, at = small_of(at, fc2_bias)
    own_bias_up = lax.dynamic_index_in_dim(
        bias_up.reshape(wide_groups, MLP, own_units), index % MLP, 1, keepdims=False
    ).reshape(up_cols)
    query_bias = lax.dynamic_slice_in_dim(bias_mixed, rank * lanes, lanes)
    value_bias = lax.dynamic_slice_in_dim(bias_mixed, width + rank * lanes, lanes)

    cotangent = jnp.stack(trade(tie(output_cotangent, "cotangent", mixed=mixed_sent, all=mixed_all, x=hidden)))

    qkv_bias = jnp.concatenate([query_bias, jnp.zeros((lanes,), f32), value_bias])
    ctx_sent, log_total, hat_one, normed_one, qkv = attention_forward(
        pos, slopes, hidden_all, gain_one, shift_one, w_mixed, qkv_bias, heads, head_size
    )
    ctx_parts = to_ranks(ctx_sent.reshape(ranks, 2 * rows, lanes))
    context = ctx_parts.transpose(1, 0, 2).reshape(2, rows, width)
    there = dict(mixed=mixed_sent, all=mixed_all, x=hidden, xa=hidden_all, ctx=ctx_sent, parts=ctx_parts)
    kinds = (
        list(range(len(leaf_bits))), list(range(len(leaf_bits), len(wide) - 1)), [len(wide) - 1]
    )

    def ordered(kind_order):
        return [wide[i] for kind in kind_order for i in kinds[kind]]

    order_up, order_down = ordered((1, 0, 2)), ordered((1, 2, 0))
    up_weight = grow(opened(up_sent, wide), order_up, "up_", **there).reshape(width, up_cols)
    down_weight = grow(opened(fc2_weight, wide), order_down, "down_", **there).reshape(up_cols, width)
    cotangent_all = gather_near(tie(cotangent, "near", **there).reshape(2 * rows, width))
    branch_out = jnp.einsum("mrd,de->mre", context, w_output, preferred_element_type=f32)
    middle = hidden.astype(f32) + (branch_out + bias_output)
    hat_two, inverse_two = normalize(middle)
    normed_two = (hat_two * gain_two + shift_two).astype(bf16)
    normed_all = gather_near(normed_two.reshape(2 * rows, width))

    normed_all, cotangent_all = jnp.stack(normed_all), jnp.stack(cotangent_all)
    expand = jnp.einsum("brd,df->brf", normed_all, up_weight, preferred_element_type=f32)
    expand = expand + own_bias_up
    root = (2.0 / jnp.pi) ** 0.5
    square = expand * expand
    tanh = jnp.tanh(root * (expand + 0.044715 * square * expand))
    active = (0.5 * expand * (1.0 + tanh)).astype(bf16)
    slope = 0.5 * (1.0 + tanh) + 0.5 * expand * (1.0 - tanh * tanh) * root * (
        1.0 + 3 * 0.044715 * square
    )
    grad_active = jnp.einsum("brd,fd->brf", cotangent_all, down_weight, preferred_element_type=f32)
    grad_expand = (grad_active * slope).astype(bf16)
    grad_normed_part = jnp.einsum(
        "brf,df->brd", grad_expand, up_weight, preferred_element_type=f32
    ).astype(bf16)
    grad_normed_two = scatter_near(grad_normed_part)
    g_bias_up = jnp.sum(grad_expand, axis=(0, 1), dtype=f32)
    grad_first = grad_normed_part
    grad_normed_two = grad_normed_two.reshape(2, rows, width)

    reduced_part = jnp.einsum(
        "brf,fd->brd", tie(active, "reduced", g=grad_normed_two, p=grad_first), down_weight, preferred_element_type=f32
    ).astype(bf16)
    reduced = scatter_near(tie(reduced_part, "reduced_sent", g=grad_normed_two)).reshape(2, rows, width)
    g_down = jnp.einsum(
        "brf,brd->fd", tie(active, "down_made", g=grad_normed_two, p=grad_first), cotangent_all, preferred_element_type=f32
    ).astype(bf16)
    g_up = jnp.einsum(
        "brd,brf->df", normed_all, tie(grad_expand, "up_made", g=grad_normed_two, p=grad_first), preferred_element_type=f32
    ).astype(bf16)
    cot = cotangent.astype(f32)
    g_gain_two = jnp.sum(grad_normed_two * hat_two, axis=(0, 1))
    g_shift_two = jnp.sum(grad_normed_two, axis=(0, 1))
    g_bias_down = jnp.sum(cot, axis=(0, 1))
    grad_middle = cot + norm_back(hat_two, inverse_two, gain_two, grad_normed_two)
    grad_branch = grad_middle.astype(bf16)
    g_bias_output = jnp.sum(grad_branch, axis=(0, 1), dtype=f32)
    grad_context = jnp.einsum(
        "mre,de->mrd", grad_branch, w_output, preferred_element_type=f32
    ).astype(bf16)
    gctx_sent = grad_context.reshape(2 * rows, ranks, lanes).transpose(1, 0, 2)
    gctx_parts = to_ranks(gctx_sent).reshape(2 * ranks, rows, lanes)
    g_output = jnp.einsum("mrd,mre->de", context, grad_branch, preferred_element_type=f32)

    weight_t = w_mixed.T
    grad_projected, grad_sent, g_gain_far, g_shift_far = attention_backward(
        pos, back, slopes, qkv, log_total, gctx_parts, hat_one, weight_t, heads, head_size
    )
    grad_kept, g_gain_near, g_shift_near = project_own(back, grad_projected, hat_one, weight_t)
    g_gain_one = jnp.sum(g_gain_far + g_gain_near, axis=0)
    g_shift_one = jnp.sum(g_shift_far + g_shift_near, axis=0)
    held = (grad_kept.astype(f32) + swap(grad_sent, "tok", 1).astype(f32)).astype(bf16)
    pieces = [held[: held.shape[0] // 2], held[held.shape[0] // 2 :]]
    steps = [held]
    passes = list(zip(*[route[::-1] for route in routes(ranks)]))
    for m_own, m_other in passes:
        kind = f32 if pieces[0].shape[0] == 2 else bf16
        k = pieces[0].shape[0] // 2
        pieces = [
            (piece[:k].astype(f32) + swap(piece[k:].astype(bf16), "tok", m).astype(f32)).astype(kind)
            for piece, m in zip(pieces, (m_own, m_other))
        ]
        steps.append(pieces[1])
    grad_one = jnp.concatenate(pieces, axis=0)
    hat_own, inverse_own = normalize(hidden.astype(f32))
    input_half = (grad_middle + norm_back(hat_own, inverse_own, gain_one, grad_one)).astype(bf16)
    input_grad = trade_back(input_half[0], input_half[1])

    there = dict(
        g=grad_normed_two, gc=grad_context, gp=gctx_parts, ke=grad_sent, held=steps[0], s2=steps[1], s3=steps[-1],
    )
    back_down, back_up = ordered((0, 2, 1)), ordered((2, 0, 1))
    finished = (middle + (reduced + bias_down)).astype(bf16)
    layer_out = trade_back(finished[0], tie(finished[1], "layer_out", **there))
    g_down_own = shrink(
        split(g_down.reshape(wide_groups, own_units, width), wide), back_down, "down_back_", **there
    ).reshape(own_units, width).astype(f32)
    g_up_parts = shrink(
        split(g_up.reshape(wide_groups, MLP, weight_rows, up_cols), wide), back_up, "up_back_", **there
    ).reshape(MLP, weight_rows, up_cols)
    g_up_own = (
        to_ranks(tie(g_up_parts.astype(bf16), "up_back", **there), mlp_groups)
        .reshape(MLP, weight_rows, wide_groups, own_units)
        .transpose(1, 2, 0, 3)
        .reshape(weight_rows, hidden_units)
        .astype(f32)
    )
    g_output_parts = (
        tie(g_output, "output_sum", **there)
        .reshape(groups, ranks, weight_rows, width)
        .transpose(1, 0, 2, 3)
        .astype(bf16)
        .reshape(ranks * groups * weight_rows, width)
    )
    g_output_group = lax.psum_scatter(
        g_output_parts, "tok", scatter_dimension=0, tiled=True, axis_index_groups=rank_groups
    )
    g_output_own = shrink(
        split(tie(g_output_group, "output_own", **there).reshape(groups, weight_rows, width), narrow), turned(True), "output_back_", **there
    ).reshape(weight_rows, width).astype(f32)

    mixed_from = tie(grad_projected, "mixed_made", **there)
    g_mixed, g_bias_mixed = mixed_gradient(normed_one, mixed_from)
    g_bias_mixed = jnp.sum(g_bias_mixed, axis=0)
    own_lane = jnp.arange(ranks, dtype=jnp.int32)[:, None] == rank
    own_slice = jnp.arange(MLP, dtype=jnp.int32)[:, None] == index % MLP
    g_bias_query = jnp.where(own_lane, g_bias_mixed[None, :lanes], 0.0).reshape(-1)
    g_bias_value = jnp.where(own_lane, g_bias_mixed[None, 2 * lanes :], 0.0).reshape(-1)
    g_bias_up_all = jnp.where(
        own_slice[None], g_bias_up.reshape(wide_groups, 1, own_units), 0.0
    ).reshape(-1)
    pieces = [
        g_gain_one, g_shift_one, jnp.concatenate([g_bias_query, g_bias_value]), g_bias_output,
        g_gain_two, g_shift_two, g_bias_up_all, g_bias_down,
    ]
    sizes = [p.shape[0] // (groups * ranks) for p in pieces]
    g_small = jnp.concatenate([p.reshape(groups, ranks, -1) for p in pieces], axis=2)
    g_small = jnp.pad(g_small, ((0, 0), (0, 0), (0, small_rows * mixed_cols - g_small.shape[2])))
    g_sent = jnp.concatenate(
        [
            g_mixed.reshape(groups, ranks, weight_rows, mixed_cols),
            g_small.reshape(groups, ranks, small_rows, mixed_cols),
        ],
        axis=2,
    ).astype(bf16)
    g_held = shrink(split(g_sent, narrow), turned(True), "mixed_back_", **there)
    g_back = to_ranks(
        tie(g_held.astype(bf16), "mixed_back", **there).reshape(
            ranks, weight_rows + small_rows, mixed_cols
        )
    )
    g_mixed_own = (
        g_back[:, :weight_rows]
        .reshape(ranks, weight_rows, 3, lanes)
        .transpose(1, 2, 0, 3)
        .reshape(weight_rows, 3 * width)
        .astype(f32)
    )
    small_sum = jnp.sum(g_back[:, weight_rows:].astype(f32), axis=0).reshape(-1)
    found, at = [], 0
    for size in sizes:
        found.append(small_sum[at : at + size])
        at += size
    (
        o_gain_one, o_shift_one, o_bias_mixed, o_bias_output, o_gain_two, o_shift_two, o_bias_up,
        o_bias_down,
    ) = found
    return (
        layer_out, input_grad, o_gain_one, o_shift_one, g_mixed_own, o_bias_mixed, g_output_own,
        o_bias_output, o_gain_two, o_shift_two, g_up_own, o_bias_up, g_down_own, o_bias_down,
    )


def solution(mesh):
    both = ("leaf", "tok")
    tokens, matrix, vector = P("leaf", "tok", None), P(both, None), P(both)
    return jax.shard_map(
        on_device,
        mesh=mesh,
        in_specs=(
            tokens, tokens, P("leaf", None), vector, vector, matrix, vector, matrix, vector, vector,
            vector, matrix, vector, matrix, vector,
        ),
        out_specs=(
            tokens, tokens, vector, vector, matrix, vector, matrix, vector, vector, vector, matrix,
            vector, matrix, vector,
        ),
        check_vma=False,
    )
```

```python
import jax
import jax.numpy as jnp
from jax import lax
from jax.experimental import pallas as pl
from jax.experimental.pallas import tpu as pltpu
from jax.sharding import PartitionSpec as P

HEADS = 16
UNITS = 16
LOG2E = 1.4426950408889634
WAITS = {
    "down_o0": "xa",
    "down_v0": "mixed",
    "output_back_o0": "held",
    "up_o1": "xa",
}


def tie(value, name, **there):
    key = WAITS.get(name)
    return after(value, there[key]) if key else value


layer_eps = 1e-05
masked_score = -1e30
f32 = jnp.float32
bf16 = jnp.bfloat16


def normalize(values):
    row_mean = jnp.mean(values, axis=-1, keepdims=True)
    centered = values - row_mean
    spread = jnp.mean(centered * centered, axis=-1, keepdims=True)
    inverse = lax.rsqrt(spread + layer_eps)
    return centered * inverse, inverse


def norm_back(hat, inverse, gain, grad):
    scaled = grad * gain
    first = jnp.mean(scaled, axis=-1, keepdims=True)
    second = jnp.mean(scaled * hat, axis=-1, keepdims=True)
    return (scaled - first - hat * second) * inverse


def fill_transposed(src, dst, unit_len):
    for u in range(UNITS):
        dst[:, u * unit_len : (u + 1) * unit_len] = (
            src[u * unit_len : (u + 1) * unit_len, :].astype(f32).T.astype(bf16)
        )


def head_stack(block, heads, head_size):
    if heads == 1:
        return block
    lane = lax.broadcasted_iota(jnp.int32, block.shape, 1) // head_size
    return jnp.concatenate(
        [jnp.where(lane == h, block, jnp.zeros_like(block)) for h in range(heads)], axis=0
    )


def fill_bias(slope_ref, bias_ref, heads, unit_len):
    depth = lax.broadcasted_iota(jnp.int32, (bias_ref.shape[0], unit_len), 0).astype(f32)
    for h in range(heads):
        bias_ref[:, h * unit_len : (h + 1) * unit_len] = depth * slope_ref[h]


def nt_dot(left, right):
    return lax.dot_general(left, right, (((1,), (1,)), ((), ())), preferred_element_type=f32)


def nn_dot(left, right):
    return lax.dot_general(left, right, (((1,), (0,)), ((), ())), preferred_element_type=f32)


def diag_of(wide, heads, head_size, unit_len):
    return jnp.concatenate(
        [
            wide[h * head_size : (h + 1) * head_size, h * unit_len : (h + 1) * unit_len]
            for h in range(heads)
        ],
        axis=0,
    )


def over_units(unit_len, one_unit):
    for u in range(4):
        pieces = [(u * unit_len, unit_len, u * unit_len, True)]
        if u:
            pieces = [(0, u * unit_len, 0, False)] + pieces
        one_unit(u * unit_len, pieces)

    def branch(b, carry):
        start = pl.multiple_of((4 + b) * unit_len, unit_len)
        one_unit(
            start, [(0, 4 * unit_len, 0, False), (start, unit_len, 4 * unit_len, True)]
        )
        return carry

    lax.fori_loop(0, 4, branch, 0, unroll=4)

    def leaf(k, carry):
        start = pl.multiple_of((8 + k) * unit_len, unit_len)
        parent = pl.multiple_of((4 + k // 2) * unit_len, unit_len)
        one_unit(
            start,
            [
                (0, 4 * unit_len, 0, False),
                (parent, unit_len, 4 * unit_len, False),
                (start, unit_len, 5 * unit_len, True),
            ],
        )
        return carry

    lax.fori_loop(0, 8, leaf, 0, unroll=8)


def forward_kernel(
    pos_ref, slope_ref, x_ref, gain_ref, shift_ref, w_ref, qb_ref, ctx_ref, log_ref, hat_out,
    normed_out, qkv_out, hat_s, normed_s, qkv_s, vt_s, bias_s, c_s, sems, *, heads, head_size
):
    width = heads * head_size
    blocks, rows, model = x_ref.shape
    unit_len = blocks * rows // UNITS
    gain, shift = gain_ref[...], shift_ref[...]
    q_s, k_s, v_s = qkv_s.at[0], qkv_s.at[1], qkv_s.at[2]

    def out_copies(n):
        part = pl.ds(2 * n, 2)
        return (
            pltpu.make_async_copy(hat_s.at[part], hat_out.at[part], sems.at[0, n]),
            pltpu.make_async_copy(normed_s.at[part], normed_out.at[part], sems.at[1, n]),
        )

    for n in range(blocks // 2):
        values = x_ref[2 * n : 2 * n + 2].reshape(2 * rows, model).astype(f32)
        hat, _ = normalize(values)
        normed = (hat * gain + shift).astype(bf16)
        hat_s[2 * n : 2 * n + 2] = hat.astype(bf16).reshape(2, rows, model)
        normed_s[2 * n : 2 * n + 2] = normed.reshape(2, rows, model)
        for copy in out_copies(n):
            copy.start()
        made = (nn_dot(normed, w_ref[...]) + qb_ref[...]).astype(bf16)
        for i in range(2):
            dst = pl.ds(pl.multiple_of(pos_ref[2 * n + i], rows), rows)
            for m in range(3):
                qkv_s[m, dst, :] = made[i * rows : (i + 1) * rows, m * width : (m + 1) * width]
    qkv_copy = pltpu.make_async_copy(qkv_s, qkv_out, sems.at[2, 0])
    qkv_copy.start()
    fill_transposed(v_s, vt_s, unit_len)
    fill_bias(slope_ref, bias_s, heads, unit_len)
    scale = head_size ** (-0.5) * LOG2E
    columns = heads * unit_len
    key_row = lax.broadcasted_iota(jnp.int32, (unit_len, columns), 0)
    query_col = lax.broadcasted_iota(jnp.int32, (unit_len, columns), 1) % unit_len
    causal = key_row <= query_col

    def one_unit(start, pieces):
        stacked = head_stack(q_s[pl.ds(start, unit_len), :], heads, head_size)
        scores = []
        top = None
        for key_start, size, depth, diagonal in pieces:
            s = nt_dot(k_s[pl.ds(key_start, size), :], stacked) * scale
            s = s + bias_s[depth : depth + size, :]
            if diagonal:
                s = jnp.where(causal, s, masked_score)
            scores.append(s)
            m = jnp.max(s, axis=0, keepdims=True)
            top = m if top is None else jnp.maximum(top, m)
        total = None
        wide = None
        for (key_start, size, depth, diagonal), s in zip(pieces, scores):
            p = jnp.exp2(s - top)
            part = jnp.sum(p, axis=0, keepdims=True)
            total = part if total is None else total + part
            o = nn_dot(vt_s[:, pl.ds(key_start, size)], p.astype(bf16))
            wide = o if wide is None else wide + o
        wide = wide * (1.0 / total)
        log_ref[pl.ds(start // unit_len, 1), :] = top + jnp.log2(total)
        c_s[pl.ds(start, unit_len), :] = diag_of(wide, heads, head_size, unit_len).T.astype(bf16)

    over_units(unit_len, one_unit)
    for i in range(blocks):
        src = pl.ds(pl.multiple_of(pos_ref[i], rows), rows)
        ctx_ref[i, :, :] = c_s[src, :]
    for n in range(blocks // 2):
        for copy in out_copies(n):
            copy.wait()
    qkv_copy.wait()


def project_back(back_ref, first_block, out_ref, hat_ref, wt_ref, grad_ref, gain_ref, shift_ref):
    count, rows, model = grad_ref.shape
    gain_ref[...] = jnp.zeros_like(gain_ref)
    shift_ref[...] = jnp.zeros_like(shift_ref)
    for n in range(0, count, 2):
        first, second = back_ref[first_block + n], back_ref[first_block + n + 1]
        rows_in = jnp.concatenate([out_ref[first], out_ref[second]], axis=0)
        grad = nt_dot(rows_in, wt_ref[...])
        grad_ref[n : n + 2] = grad.astype(bf16).reshape(2, rows, model)
        hat = jnp.concatenate([hat_ref[first], hat_ref[second]], axis=0).astype(f32)
        gain_ref[...] += jnp.sum((grad * hat).reshape(-1, 8, model), axis=0)
        shift_ref[...] += jnp.sum(grad.reshape(-1, 8, model), axis=0)


def project_kernel(back_ref, out_ref, hat_ref, wt_ref, grad_ref, gain_ref, shift_ref):
    project_back(back_ref, 0, out_ref, hat_ref, wt_ref, grad_ref, gain_ref, shift_ref)


def backward_kernel(
    pos_ref, back_ref, slope_ref, qkv_in, log_ref, gctx_ref, hat_in, wt_ref,
    out_ref, grad_ref, gain_ref, shift_ref,
    qkv_s, hat_s, kt_s, g_s, bias_s, dq_s, dk_s, dv_s, sems, *, heads, head_size
):
    width = heads * head_size
    blocks, rows, model = hat_in.shape
    unit_len = blocks * rows // UNITS
    qkv_copy = pltpu.make_async_copy(qkv_in, qkv_s, sems.at[0])
    qkv_copy.start()
    hat_copy = pltpu.make_async_copy(hat_in, hat_s, sems.at[1])
    hat_copy.start()
    q_s, k_s, v_s = qkv_s.at[0], qkv_s.at[1], qkv_s.at[2]
    for i in range(blocks):
        dst = pl.ds(pl.multiple_of(pos_ref[i], rows), rows)
        g_s[dst, :] = gctx_ref[i, :, :]
    qkv_copy.wait()
    fill_transposed(k_s, kt_s, unit_len)
    fill_bias(slope_ref, bias_s, heads, unit_len)
    dk_s[...] = jnp.zeros_like(dk_s)
    dv_s[...] = jnp.zeros_like(dv_s)
    size_scale = head_size ** (-0.5)
    scale = size_scale * LOG2E
    columns = heads * unit_len
    key_row = lax.broadcasted_iota(jnp.int32, (unit_len, columns), 0)
    query_col = lax.broadcasted_iota(jnp.int32, (unit_len, columns), 1) % unit_len
    causal = key_row <= query_col

    def one_unit(start, pieces):
        stacked = head_stack(q_s[pl.ds(start, unit_len), :], heads, head_size)
        grads = head_stack(g_s[pl.ds(start, unit_len), :], heads, head_size)
        log_total = log_ref[pl.ds(start // unit_len, 1), :]
        kept = []
        delta = None
        for key_start, size, depth, diagonal in pieces:
            s = nt_dot(k_s[pl.ds(key_start, size), :], stacked) * scale
            s = s + bias_s[depth : depth + size, :]
            if diagonal:
                s = jnp.where(causal, s, masked_score)
            p = jnp.exp2(s - log_total)
            gp = nt_dot(v_s[pl.ds(key_start, size), :], grads)
            kept.append((p, gp))
            part = jnp.sum(p * gp, axis=0, keepdims=True)
            delta = part if delta is None else delta + part
        wide = None
        for (key_start, size, depth, diagonal), (p, gp) in zip(pieces, kept):
            ds = (p * (gp - delta)).astype(bf16)
            keys = pl.ds(key_start, size)
            dv_s[keys, :] += nn_dot(p.astype(bf16), grads)
            dk_s[keys, :] += nn_dot(ds, stacked)
            o = nn_dot(kt_s[:, keys], ds)
            wide = o if wide is None else wide + o
        dq = diag_of(wide, heads, head_size, unit_len).T * size_scale
        dq_s[pl.ds(start, unit_len), :] = dq.astype(bf16)

    over_units(unit_len, one_unit)
    for i in range(blocks):
        src = pl.ds(pl.multiple_of(pos_ref[i], rows), rows)
        out_ref[i, :, :width] = dq_s[src, :]
        out_ref[i, :, width : 2 * width] = (dk_s[src, :] * size_scale).astype(bf16)
        out_ref[i, :, 2 * width :] = dv_s[src, :].astype(bf16)
    hat_copy.wait()
    project_back(back_ref, blocks // 2, out_ref, hat_s, wt_ref, grad_ref, gain_ref, shift_ref)


def memory_specs(count, kind):
    return [pl.BlockSpec(memory_space=kind)] * count


def attention_forward(pos, slopes, hidden, gain, shift, weight, bias, heads, head_size):
    blocks, rows, model = hidden.shape
    tokens, width = blocks * rows, heads * head_size
    unit_len = tokens // UNITS
    whole = jax.ShapeDtypeStruct((blocks, rows, model), bf16)
    return pl.pallas_call(
        lambda *refs: forward_kernel(*refs, heads=heads, head_size=head_size),
        out_shape=(
            jax.ShapeDtypeStruct((blocks, rows, width), bf16),
            jax.ShapeDtypeStruct((UNITS, heads * unit_len), f32),
            whole, whole, jax.ShapeDtypeStruct((3, tokens, width), bf16),
        ),
        in_specs=memory_specs(2, pltpu.SMEM) + memory_specs(5, pltpu.VMEM),
        out_specs=tuple(memory_specs(2, pltpu.VMEM) + memory_specs(3, pltpu.HBM)),
        scratch_shapes=[
            pltpu.VMEM((blocks, rows, model), bf16), pltpu.VMEM((blocks, rows, model), bf16),
            pltpu.VMEM((3, tokens, width), bf16), pltpu.VMEM((width, tokens), bf16),
            pltpu.VMEM((6 * unit_len, heads * unit_len), f32), pltpu.VMEM((tokens, width), bf16),
            pltpu.SemaphoreType.DMA((3, blocks // 2)),
        ],
        compiler_params=pltpu.CompilerParams(vmem_limit_bytes=60 * 2**20),
        cost_estimate=pl.CostEstimate(
            flops=2000000000, bytes_accessed=2**20, transcendentals=0,
        ),
    )(pos, slopes, hidden, gain[None], shift[None], weight, bias[None])


def attention_backward(
    pos, back, slopes, qkv, log_total, gctx, hat, weight_t, heads, head_size
):
    blocks, rows, model = hat.shape
    tokens, width = blocks * rows, heads * head_size
    unit_len = tokens // UNITS
    seq = lambda: pltpu.VMEM((tokens, width), bf16)
    acc = lambda: pltpu.VMEM((tokens, width), f32)
    hbm, vmem = memory_specs(1, pltpu.HBM), memory_specs(1, pltpu.VMEM)
    return pl.pallas_call(
        lambda *refs: backward_kernel(*refs, heads=heads, head_size=head_size),
        out_shape=(
            jax.ShapeDtypeStruct((blocks, rows, 3 * width), bf16),
            jax.ShapeDtypeStruct((blocks // 2, rows, model), bf16),
            jax.ShapeDtypeStruct((8, model), f32),
            jax.ShapeDtypeStruct((8, model), f32),
        ),
        in_specs=memory_specs(3, pltpu.SMEM) + hbm + vmem * 2 + hbm + vmem,
        out_specs=tuple(vmem * 4),
        scratch_shapes=[
            pltpu.VMEM((3, tokens, width), bf16), pltpu.VMEM((blocks, rows, model), bf16),
            pltpu.VMEM((width, tokens), bf16), seq(),
            pltpu.VMEM((6 * unit_len, heads * unit_len), f32), seq(), acc(), acc(),
            pltpu.SemaphoreType.DMA((2,)),
        ],
        compiler_params=pltpu.CompilerParams(vmem_limit_bytes=48 * 2**20),
        cost_estimate=pl.CostEstimate(
            flops=2000000000, bytes_accessed=2**20, transcendentals=0,
        ),
    )(pos, back, slopes, qkv, log_total, gctx, hat, weight_t)


def project_own(back, grad_projected, hat, weight_t):
    blocks, rows, model = hat.shape
    return pl.pallas_call(
        project_kernel,
        out_shape=(
            jax.ShapeDtypeStruct((blocks // 2, rows, model), bf16),
            jax.ShapeDtypeStruct((8, model), f32),
            jax.ShapeDtypeStruct((8, model), f32),
        ),
        in_specs=memory_specs(1, pltpu.SMEM) + memory_specs(3, pltpu.VMEM),
        out_specs=tuple(memory_specs(3, pltpu.VMEM)),
        compiler_params=pltpu.CompilerParams(vmem_limit_bytes=24 * 2**20),
        cost_estimate=pl.CostEstimate(
            flops=2000000000, bytes_accessed=2**20, transcendentals=0,
        ),
    )(back, grad_projected, hat, weight_t)


def call(body, outs, inputs, scratch=(), smem=0, limit=60, hbm_out=()):
    specs = memory_specs(smem, pltpu.SMEM) + memory_specs(len(inputs) - smem, pltpu.VMEM)
    return pl.pallas_call(
        body,
        out_shape=tuple(outs),
        in_specs=specs,
        out_specs=tuple(memory_specs(len(outs), pltpu.VMEM)),
        scratch_shapes=list(scratch),
        compiler_params=pltpu.CompilerParams(vmem_limit_bytes=limit * 2**20),
        cost_estimate=pl.CostEstimate(flops=2**20, bytes_accessed=2**20, transcendentals=0),
    )(*inputs)


def shaped(shape, kind=bf16):
    return jax.ShapeDtypeStruct(shape, kind)


def tn_dot(left, right):
    return lax.dot_general(left, right, (((0,), (0,)), ((), ())), preferred_element_type=f32)


def mixed_kernel(normed_ref, grad_ref, out_ref, sum_ref):
    blocks, rows, width = normed_ref.shape
    grads = grad_ref[...].reshape(blocks * rows, -1)
    sum_ref[...] = jnp.sum(grads.astype(f32).reshape(-1, 8, grads.shape[1]), axis=0)
    for i in range(0, width, 256):
        part = tn_dot(normed_ref[:, :, i : i + 256].reshape(blocks * rows, 256), grads)
        out_ref[i : i + 256, :] = part.astype(bf16)


def mixed_gradient(normed, grads):
    return call(
        mixed_kernel,
        (shaped((normed.shape[2], grads.shape[2])), shaped((8, grads.shape[2]), f32)),
        (normed, grads), limit=24,
    )


def swap(values, axis, mask):
    size = lax.axis_size(axis)
    return lax.ppermute(values, axis, [(i, i ^ mask) for i in range(size)])


def masks_of(size):
    found, mask = [], 1
    while mask < size:
        found.append(mask)
        mask *= 2
    return found


def pick(values, dim, high):
    low, up = lax.index_in_dim(values, 0, dim, False), lax.index_in_dim(values, 1, dim, False)
    return jnp.where(high, up, low), jnp.where(high, low, up)


def grow(values, bits, name="", **there):
    for n, (axis, mask, dim) in enumerate(bits):
        values = tie(values, name + f"v{n}", **there)
        other = tie(swap(values, axis, mask), name + f"o{n}", **there)
        high = (lax.axis_index(axis) & mask) != 0
        values = jnp.concatenate(
            [jnp.where(high, other, values), jnp.where(high, values, other)], axis=dim
        )
    return values


def shrink(values, bits, name="", **there):
    for n, (axis, mask, dim) in enumerate(bits):
        values = tie(values, name + f"v{n}", **there)
        keep, send = pick(values, dim, (lax.axis_index(axis) & mask) != 0)
        other = tie(swap(send.astype(bf16), axis, mask), name + f"o{n}", **there)
        values = jnp.expand_dims((keep.astype(f32) + other.astype(f32)).astype(bf16), dim)
    return values


def routes(ranks):
    far = [m for m in masks_of(ranks) if m > 1]
    return far[::-1], far


def block_order(ranks):
    order = []
    for half, masks in enumerate(routes(ranks)):
        seen = [0]
        for m in masks:
            seen = seen + [j ^ m for j in seen]
        order += [(j, half) for j in seen]
    return order + [(j ^ 1, half) for j, half in order]


def after(value, *needed):
    return lax.optimization_barrier((value,) + needed)[0]


MLP = 4


def gather_near(block):
    far = swap(block, "tok", 2)
    near = swap(block, "tok", 1)
    return [block, near, far, swap(far, "tok", 1)]


def scatter_near(partial):
    pairs = partial.reshape((2, 2) + partial.shape[1:])
    held = pairs[:, 0].astype(f32) + swap(pairs[:, 1].astype(bf16), "tok", 1).astype(f32)
    return held[0] + swap(held[1].astype(bf16), "tok", 2).astype(f32)


def on_device(
    hidden_in, output_cotangent, unit_place, ln1_gain, ln1_bias, qkv_weight, qv_bias, out_weight,
    out_bias, ln2_gain, ln2_bias, fc1_weight, fc1_bias, fc2_weight, fc2_bias,
):
    trees, rows, width = hidden_in.shape
    tok_size, leaf_size = lax.axis_size("tok"), lax.axis_size("leaf")
    ranks = tok_size // trees
    head_size = width // HEADS
    heads = HEADS // ranks
    lanes = heads * head_size
    hidden_units = fc1_weight.shape[1]
    own_units = fc1_bias.shape[0]
    weight_rows = qkv_weight.shape[0]
    groups = leaf_size * trees
    wide_groups = leaf_size * tok_size // MLP
    tokens = rows * tok_size
    unit_len = tokens // UNITS
    index = lax.axis_index("tok")
    tree, rank = index // ranks, index % ranks
    rank_groups = [[g * ranks + i for i in range(ranks)] for g in range(trees)]

    def trade(values):
        own = jnp.where(tree == 0, values[0], values[1])
        return own, swap(jnp.where(tree == 0, values[1], values[0]), "tok", ranks)

    def trade_back(own, away):
        other = swap(away, "tok", ranks)
        return jnp.stack([jnp.where(tree == 0, own, other), jnp.where(tree == 0, other, own)])

    mlp_groups = [[g * MLP + i for i in range(MLP)] for g in range(tok_size // MLP)]

    def to_ranks(values, among=rank_groups):
        return lax.all_to_all(values, "tok", 0, 0, tiled=True, axis_index_groups=among)

    leaf_bits = [("leaf", m) for m in masks_of(leaf_size)[::-1]]
    tok_bits = [("tok", m) for m in masks_of(tok_size)[::-1]]
    tree_bits = [b for b in tok_bits if b[1] >= ranks]
    high_bits = [b for b in tok_bits if b[1] >= MLP]
    narrow = [b + (d,) for d, b in enumerate(leaf_bits + tree_bits)]
    wide = [b + (d,) for d, b in enumerate(leaf_bits + high_bits)]
    leaves = len(leaf_bits)
    wide_leaf, wide_tok = wide[:leaves], wide[leaves:]
    route_a = wide_tok + wide_leaf
    route_b = wide_tok[:-1] + wide_leaf + wide_tok[-1:]

    def turned(leaf_first):
        return list(narrow) if leaf_first else narrow[leaves:] + narrow[:leaves]

    def opened(values, bits):
        return values.reshape((1,) * len(bits) + values.shape)

    def split(values, bits):
        return values.reshape((2,) * len(bits) + values.shape[1:])

    half = tree ^ (jnp.arange(2 * ranks, dtype=jnp.int32) % 2)
    peer = jnp.arange(2 * ranks, dtype=jnp.int32) // 2
    order = block_order(ranks)
    back = (rank ^ jnp.array([j for j, _ in order], jnp.int32)) * 2 + jnp.array(
        [h for _, h in order], jnp.int32
    )
    position = (half * ranks + peer) * rows
    place = jnp.where(tree == 0, unit_place[0], unit_place[1])
    slot = position // unit_len
    unit_at = jnp.sum(
        jnp.where(slot[:, None] == jnp.arange(UNITS, dtype=jnp.int32)[None, :], place[None, :], 0),
        axis=1,
    )
    pos = unit_at * unit_len + position % unit_len
    head_index = (rank * heads + jnp.arange(heads, dtype=jnp.int32)).astype(f32)
    slopes = jnp.exp2(-8.0 * (head_index + 1.0) / HEADS) * LOG2E

    vectors = [ln1_gain, ln1_bias, qv_bias, out_bias, ln2_gain, ln2_bias, fc1_bias, fc2_bias]
    small_size = sum(v.shape[0] for v in vectors)
    mixed_cols = 3 * lanes
    small_rows = -(-small_size // mixed_cols)
    small_block, at = jnp.zeros((small_rows * mixed_cols,), bf16), 0
    for v in vectors:
        small_block += jnp.pad(v, (at, small_rows * mixed_cols - at - v.shape[0]))
        at += v.shape[0]
    small_block = jnp.broadcast_to(
        small_block.reshape(1, small_rows, mixed_cols), (ranks, small_rows, mixed_cols)
    )
    mixed_parts = (
        qkv_weight.reshape(weight_rows, 3, ranks, lanes)
        .transpose(2, 0, 1, 3)
        .reshape(ranks, weight_rows, mixed_cols)
    )
    up_cols = wide_groups * own_units
    up_parts = (
        fc1_weight.reshape(weight_rows, wide_groups, MLP, own_units)
        .transpose(2, 0, 1, 3)
        .reshape(MLP, weight_rows, up_cols)
    )
    mixed_sent = to_ranks(jnp.concatenate([mixed_parts, small_block], axis=1))
    hidden = tie(jnp.stack(trade(hidden_in)), "input", mixed=mixed_sent)
    hidden_all = lax.all_gather(
        hidden, "tok", axis=0, tiled=True, axis_index_groups=rank_groups
    )
    mixed_all = grow(opened(mixed_sent, narrow), turned(False)).reshape(
        groups, ranks, weight_rows + small_rows, mixed_cols
    )
    w_mixed = mixed_all[:, :, :weight_rows].reshape(width, mixed_cols)
    smalls = mixed_all[:, :, weight_rows:].reshape(groups * ranks, small_rows * mixed_cols)
    up_sent = to_ranks(tie(up_parts, "up", mixed=mixed_sent, all=mixed_all, x=hidden), mlp_groups)
    out_rows = grow(
        opened(tie(out_weight, "output", mixed=mixed_sent, all=mixed_all, x=hidden), narrow),
        turned(False),
    ).reshape(groups * weight_rows, width)
    w_output = (
        lax.all_gather(tie(out_rows, "output_gather", all=mixed_all, x=hidden_all), "tok", axis=0, tiled=False, axis_index_groups=rank_groups)
        .reshape(ranks, groups, weight_rows, width)
        .transpose(1, 0, 2, 3)
        .reshape(width, width)
    )

    def small_of(start, array):
        n = array.shape[0]
        return smalls[:, start : start + n].reshape(-1).astype(f32), start + n

    gain_one, at = small_of(0, ln1_gain)
    shift_one, at = small_of(at, ln1_bias)
    bias_mixed, at = small_of(at, qv_bias)
    bias_output, at = small_of(at, out_bias)
    gain_two, at = small_of(at, ln2_gain)
    shift_two, at = small_of(at, ln2_bias)
    bias_up, at = small_of(at, fc1_bias)
    bias_down, at = small_of(at, fc2_bias)
    own_bias_up = lax.dynamic_index_in_dim(
        bias_up.reshape(wide_groups, MLP, own_units), index % MLP, 1, keepdims=False
    ).reshape(up_cols)
    query_bias = lax.dynamic_slice_in_dim(bias_mixed, rank * lanes, lanes)
    value_bias = lax.dynamic_slice_in_dim(bias_mixed, width + rank * lanes, lanes)

    cotangent = jnp.stack(trade(tie(output_cotangent, "cotangent", mixed=mixed_sent, all=mixed_all, x=hidden)))

    qkv_bias = jnp.concatenate([query_bias, jnp.zeros((lanes,), f32), value_bias])
    ctx_sent, log_total, hat_one, normed_one, qkv = attention_forward(
        pos, slopes, hidden_all, gain_one, shift_one, w_mixed, qkv_bias, heads, head_size
    )
    ctx_parts = to_ranks(ctx_sent.reshape(ranks, 2 * rows, lanes))
    context = ctx_parts.transpose(1, 0, 2).reshape(2, rows, width)
    there = dict(mixed=mixed_sent, all=mixed_all, x=hidden, xa=hidden_all, ctx=ctx_sent, parts=ctx_parts)
    kinds = (
        list(range(len(leaf_bits))), list(range(len(leaf_bits), len(wide) - 1)), [len(wide) - 1]
    )

    def ordered(kind_order):
        return [wide[i] for kind in kind_order for i in kinds[kind]]

    order_up, order_down = ordered((1, 0, 2)), ordered((1, 2, 0))
    up_weight = grow(opened(up_sent, wide), order_up, "up_", **there).reshape(width, up_cols)
    down_weight = grow(opened(fc2_weight, wide), order_down, "down_", **there).reshape(up_cols, width)
    cotangent_all = gather_near(tie(cotangent, "near", **there).reshape(2 * rows, width))
    branch_out = jnp.einsum("mrd,de->mre", context, w_output, preferred_element_type=f32)
    middle = hidden.astype(f32) + (branch_out + bias_output)
    hat_two, inverse_two = normalize(middle)
    normed_two = (hat_two * gain_two + shift_two).astype(bf16)
    normed_all = gather_near(normed_two.reshape(2 * rows, width))

    normed_all, cotangent_all = jnp.stack(normed_all), jnp.stack(cotangent_all)
    expand = jnp.einsum("brd,df->brf", normed_all, up_weight, preferred_element_type=f32)
    expand = expand + own_bias_up
    root = (2.0 / jnp.pi) ** 0.5
    square = expand * expand
    tanh = jnp.tanh(root * (expand + 0.044715 * square * expand))
    active = (0.5 * expand * (1.0 + tanh)).astype(bf16)
    slope = 0.5 * (1.0 + tanh) + 0.5 * expand * (1.0 - tanh * tanh) * root * (
        1.0 + 3 * 0.044715 * square
    )
    grad_active = jnp.einsum("brd,fd->brf", cotangent_all, down_weight, preferred_element_type=f32)
    grad_expand = (grad_active * slope).astype(bf16)
    grad_normed_part = jnp.einsum(
        "brf,df->brd", grad_expand, up_weight, preferred_element_type=f32
    ).astype(bf16)
    grad_normed_two = scatter_near(grad_normed_part)
    g_bias_up = jnp.sum(grad_expand, axis=(0, 1), dtype=f32)
    grad_first = grad_normed_part
    grad_normed_two = grad_normed_two.reshape(2, rows, width)

    reduced_part = jnp.einsum(
        "brf,fd->brd", tie(active, "reduced", g=grad_normed_two, p=grad_first), down_weight, preferred_element_type=f32
    ).astype(bf16)
    reduced = scatter_near(tie(reduced_part, "reduced_sent", g=grad_normed_two)).reshape(2, rows, width)
    g_down = jnp.einsum(
        "brf,brd->fd", tie(active, "down_made", g=grad_normed_two, p=grad_first), cotangent_all, preferred_element_type=f32
    ).astype(bf16)
    g_up = jnp.einsum(
        "brd,brf->df", normed_all, tie(grad_expand, "up_made", g=grad_normed_two, p=grad_first), preferred_element_type=f32
    ).astype(bf16)
    cot = cotangent.astype(f32)
    g_gain_two = jnp.sum(grad_normed_two * hat_two, axis=(0, 1))
    g_shift_two = jnp.sum(grad_normed_two, axis=(0, 1))
    g_bias_down = jnp.sum(cot, axis=(0, 1))
    grad_middle = cot + norm_back(hat_two, inverse_two, gain_two, grad_normed_two)
    grad_branch = grad_middle.astype(bf16)
    g_bias_output = jnp.sum(grad_branch, axis=(0, 1), dtype=f32)
    grad_context = jnp.einsum(
        "mre,de->mrd", grad_branch, w_output, preferred_element_type=f32
    ).astype(bf16)
    gctx_sent = grad_context.reshape(2 * rows, ranks, lanes).transpose(1, 0, 2)
    gctx_parts = to_ranks(gctx_sent).reshape(2 * ranks, rows, lanes)
    g_output = jnp.einsum("mrd,mre->de", context, grad_branch, preferred_element_type=f32)

    weight_t = w_mixed
    grad_projected, grad_sent, g_gain_far, g_shift_far = attention_backward(
        pos, back, slopes, qkv, log_total, gctx_parts, hat_one, weight_t, heads, head_size
    )
    grad_kept, g_gain_near, g_shift_near = project_own(back, grad_projected, hat_one, weight_t)
    g_gain_one = jnp.sum(g_gain_far + g_gain_near, axis=0)
    g_shift_one = jnp.sum(g_shift_far + g_shift_near, axis=0)
    held = (grad_kept.astype(f32) + swap(grad_sent, "tok", 1).astype(f32)).astype(bf16)
    pieces = [held[: held.shape[0] // 2], held[held.shape[0] // 2 :]]
    steps = [held]
    passes = list(zip(*[route[::-1] for route in routes(ranks)]))
    for m_own, m_other in passes:
        kind = f32 if pieces[0].shape[0] == 2 else bf16
        k = pieces[0].shape[0] // 2
        pieces = [
            (piece[:k].astype(f32) + swap(piece[k:].astype(bf16), "tok", m).astype(f32)).astype(kind)
            for piece, m in zip(pieces, (m_own, m_other))
        ]
        steps.append(pieces[1])
    grad_one = jnp.concatenate(pieces, axis=0)
    hat_own, inverse_own = normalize(hidden.astype(f32))
    input_half = (grad_middle + norm_back(hat_own, inverse_own, gain_one, grad_one)).astype(bf16)
    input_grad = trade_back(input_half[0], input_half[1])

    there = dict(
        g=grad_normed_two, gc=grad_context, gp=gctx_parts, ke=grad_sent, held=steps[0], s2=steps[1], s3=steps[-1],
    )
    back_down, back_up = ordered((0, 2, 1)), ordered((2, 0, 1))
    finished = (middle + (reduced + bias_down)).astype(bf16)
    layer_out = trade_back(finished[0], tie(finished[1], "layer_out", **there))
    g_down_own = shrink(
        split(g_down.reshape(wide_groups, own_units, width), wide), back_down, "down_back_", **there
    ).reshape(own_units, width).astype(f32)
    g_up_parts = shrink(
        split(g_up.reshape(wide_groups, MLP, weight_rows, up_cols), wide), back_up, "up_back_", **there
    ).reshape(MLP, weight_rows, up_cols)
    g_up_own = (
        to_ranks(tie(g_up_parts.astype(bf16), "up_back", **there), mlp_groups)
        .reshape(MLP, weight_rows, wide_groups, own_units)
        .transpose(1, 2, 0, 3)
        .reshape(weight_rows, hidden_units)
        .astype(f32)
    )
    g_output_parts = (
        tie(g_output, "output_sum", **there)
        .reshape(groups, ranks, weight_rows, width)
        .transpose(1, 0, 2, 3)
        .astype(bf16)
        .reshape(ranks * groups * weight_rows, width)
    )
    g_output_group = lax.psum_scatter(
        g_output_parts, "tok", scatter_dimension=0, tiled=True, axis_index_groups=rank_groups
    )
    g_output_own = shrink(
        split(tie(g_output_group, "output_own", **there).reshape(groups, weight_rows, width), narrow), turned(True), "output_back_", **there
    ).reshape(weight_rows, width).astype(f32)

    mixed_from = tie(grad_projected, "mixed_made", **there)
    g_mixed, g_bias_mixed = mixed_gradient(normed_one, mixed_from)
    g_bias_mixed = jnp.sum(g_bias_mixed, axis=0)
    own_lane = jnp.arange(ranks, dtype=jnp.int32)[:, None] == rank
    own_slice = jnp.arange(MLP, dtype=jnp.int32)[:, None] == index % MLP
    g_bias_query = jnp.where(own_lane, g_bias_mixed[None, :lanes], 0.0).reshape(-1)
    g_bias_value = jnp.where(own_lane, g_bias_mixed[None, 2 * lanes :], 0.0).reshape(-1)
    g_bias_up_all = jnp.where(
        own_slice[None], g_bias_up.reshape(wide_groups, 1, own_units), 0.0
    ).reshape(-1)
    pieces = [
        g_gain_one, g_shift_one, jnp.concatenate([g_bias_query, g_bias_value]), g_bias_output,
        g_gain_two, g_shift_two, g_bias_up_all, g_bias_down,
    ]
    sizes = [p.shape[0] // (groups * ranks) for p in pieces]
    g_small = jnp.concatenate([p.reshape(groups, ranks, -1) for p in pieces], axis=2)
    g_small = jnp.pad(g_small, ((0, 0), (0, 0), (0, small_rows * mixed_cols - g_small.shape[2])))
    g_sent = jnp.concatenate(
        [
            g_mixed.reshape(groups, ranks, weight_rows, mixed_cols),
            g_small.reshape(groups, ranks, small_rows, mixed_cols),
        ],
        axis=2,
    ).astype(bf16)
    g_held = shrink(split(g_sent, narrow), turned(True), "mixed_back_", **there)
    g_back = to_ranks(
        tie(g_held.astype(bf16), "mixed_back", **there).reshape(
            ranks, weight_rows + small_rows, mixed_cols
        )
    )
    g_mixed_own = (
        g_back[:, :weight_rows]
        .reshape(ranks, weight_rows, 3, lanes)
        .transpose(1, 2, 0, 3)
        .reshape(weight_rows, 3 * width)
        .astype(f32)
    )
    small_sum = jnp.sum(g_back[:, weight_rows:].astype(f32), axis=0).reshape(-1)
    found, at = [], 0
    for size in sizes:
        found.append(small_sum[at : at + size])
        at += size
    (
        o_gain_one, o_shift_one, o_bias_mixed, o_bias_output, o_gain_two, o_shift_two, o_bias_up,
        o_bias_down,
    ) = found
    return (
        layer_out, input_grad, o_gain_one, o_shift_one, g_mixed_own, o_bias_mixed, g_output_own,
        o_bias_output, o_gain_two, o_shift_two, g_up_own, o_bias_up, g_down_own, o_bias_down,
    )


def solution(mesh):
    both = ("leaf", "tok")
    tokens, matrix, vector = P("leaf", "tok", None), P(both, None), P(both)
    return jax.shard_map(
        on_device,
        mesh=mesh,
        in_specs=(
            tokens, tokens, P("leaf", None), vector, vector, matrix, vector, matrix, vector, vector,
            vector, matrix, vector, matrix, vector,
        ),
        out_specs=(
            tokens, tokens, vector, vector, matrix, vector, matrix, vector, vector, vector, matrix,
            vector, matrix, vector,
        ),
        check_vma=False,
    )
```
